32 devices in a mesh: groups: 2 (over y), bay: 4 (over z), sec: 4 (over x, core).
Axes of the slice: x: 2, y: 2, z: 4, core: 2. Of those that a mesh axis runs over, the one named last changes fastest.
Arguments:
- edge_load: bfloat16 [8, 4, 8, 3072], P(('groups', 'bay'), None, None, 'sec'), parts along dimension 0, may hold values from -6 to 6
- interior_load: bfloat16 [8, 4, 8, 3072], P(('groups', 'bay'), None, None, 'sec'), parts along dimension 0, may hold values from -6 to 6
- coupling: bfloat16 [8, 3072, 3072], P(('groups', 'bay'), 'sec'), parts along dimension 0, may hold values from -0.109375 to 0.109375
- block_cols: int32 [8, 24, 8], P(('groups', 'bay'), 'sec'), parts along dimension 0, may hold values from 0 to 23, as said below
- transfer: bfloat16 [8, 24, 8, 4, 128, 128], P(('groups', 'bay'), 'sec'), parts along dimension 0, may hold values from -0.21875 to 0.21875
- local_inverse: bfloat16 [8, 24, 4, 128, 128], P(('groups', 'bay'), 'sec'), parts along dimension 0
Outputs:
- edge_response: bfloat16 [8, 4, 8, 3072], P(('groups', 'bay'), None, None, 'sec'), parts along dimension 0
The draws below stay inside these ranges and needn't reach their ends.
There are 2 independent parts, one for each index of `groups`. The reference program is written for one: setup_inputs(seed, part) draws one part's arguments, and reference() takes and returns one part's arrays. A program takes and returns all parts, laid end to end along the dimension named above; each array names one. Nothing has to cross between parts.
Inputs may be any that keep to these rules, and one draw needn't show every extreme that they name: `block_cols`: the first entry of block row r is r itself; the 8 entries of a block row are distinct.
All inputs are finite; a program needn't handle non-finite values.
Results may differ from the reference program's by a relative error of at most 0.0074.
Values may be sent and summed in bfloat16 or wider, within the bound.
No kernel may reach another device: no remote copies, remote signals or barrier semaphores. Data moves between devices by JAX's collectives and lax.ppermute only.
A program may use at most 64 MiB of HBM per device.

```python
import jax
import jax.numpy as jnp
from jax import lax

E = 3072
BLK = 128
K = 8
F = 4
I = 3072
RC = 8
BAYS = 4
NBLK = 24


def draw_block_cols(key, part):
    row_count = E // BLK
    keys = jax.random.split(jax.random.fold_in(key, 11), BAYS * row_count)
    offsets = jax.vmap(lambda single: jax.random.permutation(single, row_count - 1)[:K - 1] + 1)(keys)
    offsets = jnp.concatenate([jnp.zeros((BAYS * row_count, 1), jnp.int32), offsets.astype(jnp.int32)], axis=1)
    row_ids = jnp.tile(jnp.arange(row_count, dtype=jnp.int32), BAYS)
    block_ids = (row_ids[:, None] + offsets) % row_count
    return block_ids.reshape(BAYS, row_count, K).astype(jnp.int32)


def draw_local_inverse(key, part):
    shape = (BAYS, E // BLK, F, BLK, BLK)
    noise = jax.random.normal(jax.random.fold_in(key, 23), shape, jnp.float32)
    values = 0.6 * jnp.eye(BLK, dtype=jnp.float32) + noise * (0.5 / BLK ** 0.5)
    return values.astype(jnp.bfloat16)


def steps_of(own_key, extent, shards, smallest, high):
    def one(position, blocks):
        draws = jax.random.uniform(jax.random.fold_in(jax.random.fold_in(own_key, 6), position), (blocks,), jnp.float32, smallest / len(shards), high / len(shards))
        return jnp.repeat(jnp.exp(draws), extent[position] // blocks).reshape((-1,) + (1,) * (len(extent) - position - 1))

    factor_of = one(*shards[0])
    for cut in shards[1:]:
        factor_of = factor_of * one(*cut)
    return factor_of


def centred(own_key, dims, scale, reach, cuts=(), held_as=jnp.bfloat16):
    array = scale * jax.random.normal(own_key, dims, jnp.float32)
    if cuts:
        array = array * steps_of(own_key, dims, cuts, -0.22, 0.18)
    return jnp.clip(array, -reach, reach).astype(held_as)


def setup_inputs(seed: int = 0, part: int = 0) -> dict:
    key_of = jax.random.split(jax.random.key(seed), 7)
    part_splits = jax.random.split(jax.random.fold_in(key_of[6], part), 7)
    return {
        "edge_load": centred(part_splits[0], (BAYS, F, RC, E), 1.0, 6.0, ((0, 4), (3, 4))),
        "interior_load": centred(part_splits[1], (BAYS, F, RC, I), 1.0, 6.0, ((0, 4), (3, 4))),
        "coupling": centred(part_splits[2], (BAYS, I, E), I ** -0.5, 0.109375, ((0, 4), (1, 4))),
        "block_cols": draw_block_cols(jax.random.fold_in(jax.random.fold_in(key_of[6], part), 71), part),
        "transfer": centred(part_splits[4], (BAYS, NBLK, K, F, BLK, BLK), (K * BLK * 2 // 3) ** -0.5, 0.21875, ((0, 4), (1, 4))),
        "local_inverse": draw_local_inverse(jax.random.fold_in(jax.random.fold_in(key_of[6], part), 71), part),
    }


def local_solve(inverse, load):
    freqs, cases, width = load.shape
    row_blocks = inverse.shape[0]
    block = inverse.shape[-1]
    pieces = load.reshape(freqs, cases, row_blocks, block).astype(jnp.float32)
    result = jnp.einsum("rfij,fcrj->fcri", inverse.astype(jnp.float32), pieces)
    return result.reshape(freqs, cases, width)


def couple(transfer, block_ids, state):
    freqs, cases, width = state.shape
    row_blocks, nonzero = block_ids.shape
    block = transfer.shape[-1]
    pieces = state.reshape(freqs, cases, width // block, block)
    picked = jnp.take(pieces, block_ids.reshape(-1), axis=2).reshape(freqs, cases, row_blocks, nonzero, block)
    result = jnp.einsum("rkfij,fcrkj->fcri", transfer.astype(jnp.float32), picked.astype(jnp.float32))
    return result.reshape(freqs, cases, row_blocks * block)


def bay_force(edge_rows, interior_rows, coupling_rows):
    freqs, cases, inner = interior_rows.shape
    interior_term = jnp.dot(interior_rows.reshape(freqs * cases, inner), coupling_rows, preferred_element_type=jnp.float32)
    return edge_rows.astype(jnp.float32) - interior_term.reshape(freqs, cases, -1)


def reference(edge_load, interior_load, coupling, block_cols, transfer, local_inverse):
    load_term = lax.map(lambda item: bay_force(item[0], item[1], item[2]), (edge_load, interior_load, coupling))
    initial = lax.map(lambda item: local_solve(item[0], item[1].astype(jnp.bfloat16)).astype(jnp.bfloat16), (local_inverse, load_term))

    def advance(previous, item):
        inverse_rows, transfer_rows, block_ids, force_rows = item
        summed = (force_rows + couple(transfer_rows, block_ids, previous)).astype(jnp.bfloat16)
        updated = local_solve(inverse_rows, summed).astype(jnp.bfloat16)
        return updated, updated

    _, edge_response = lax.scan(advance, initial[-1], (local_inverse, transfer, block_cols, load_term))
    return edge_response
```

```python
import functools

import jax
import jax.numpy as jnp
from jax import lax
from jax.experimental import pallas as pl
from jax.experimental.pallas import tpu as pltpu
from jax.sharding import PartitionSpec as P

VMEM = pl.BlockSpec(memory_space=pltpu.VMEM)
SMEM = pl.BlockSpec(memory_space=pltpu.SMEM)
ANY = pl.BlockSpec(memory_space=pl.ANY)
MIB = 1 << 20


def nt_dot(left, right):
    return lax.dot_general(left, right, (((1,), (1,)), ((), ())), preferred_element_type=jnp.float32)


def diagonal(product, freqs):
    rows, cols = product.shape[0] // freqs, product.shape[1] // freqs
    return jnp.concatenate(
        [product[f * rows:(f + 1) * rows, f * cols:(f + 1) * cols] for f in range(freqs)], axis=0
    )


def by_parity(odd, rows):
    half = rows.shape[0] // 2
    return jnp.where(odd, rows[half:], rows[:half]), jnp.where(odd, rows[:half], rows[half:])


def columns_of(coupling, owner, width):
    return coupling.at[:, pl.ds(pl.multiple_of(owner * width, width), width)]


def far_kernel(sec_ref, interior, coupling, piece2, piece3, held, sems):
    sec = sec_ref[0]
    width = held.shape[-1]
    copies = [
        pltpu.make_async_copy(columns_of(coupling, sec ^ d, width), held.at[n], sems.at[n])
        for n, d in enumerate((2, 3))
    ]
    for copy in copies:
        copy.start()
    pieces = {2: piece2, 3: piece3}
    for n, d in enumerate((2, 3)):
        copies[n].wait()
        part = -jnp.dot(interior[...], held[n], preferred_element_type=jnp.float32)
        first, second = by_parity(((sec ^ d) & 1) == 1, part)
        pieces[d][:, :width] = first.astype(jnp.bfloat16)
        pieces[d ^ 1][:, width:] = second.astype(jnp.bfloat16)


def near_kernel(
    sec_ref, interior, edge, coupling, transfer, inverse,
    piece1, own, transfer_own, transfer_out, inverse_own, inverse_out, held, sems,
):
    sec = sec_ref[0]
    width = held.shape[-1]
    odd = (sec & 1) == 1
    half = transfer.shape[2] // 2
    mine = (sec & 1) * half
    other = half - mine
    copies = [
        pltpu.make_async_copy(columns_of(coupling, sec ^ d, width), held.at[n], sems.at[n])
        for n, d in enumerate((1, 0))
    ]
    moves = [
        pltpu.make_async_copy(inverse.at[:, pl.ds(other, half)], inverse_out, sems.at[2]),
        pltpu.make_async_copy(transfer.at[:, :, pl.ds(other, half)], transfer_out, sems.at[3]),
        pltpu.make_async_copy(inverse.at[:, pl.ds(mine, half)], inverse_own, sems.at[4]),
        pltpu.make_async_copy(transfer.at[:, :, pl.ds(mine, half)], transfer_own, sems.at[5]),
    ]
    for copy in copies + moves:
        copy.start()
    copies[0].wait()
    part = -jnp.dot(interior[...], held[0], preferred_element_type=jnp.float32)
    first, second = by_parity(jnp.logical_not(odd), part)
    piece1[:, :width] = first.astype(jnp.bfloat16)
    own[:, width:] = second
    copies[1].wait()
    part = edge[...].astype(jnp.float32) - jnp.dot(
        interior[...], held[1], preferred_element_type=jnp.float32
    )
    first, second = by_parity(odd, part)
    own[:, :width] = first
    piece1[:, width:] = second.astype(jnp.bfloat16)
    for move in moves:
        move.wait()


def initial_kernel(own, got1, got2, got3, inverse_own, inverse_got, load, initial):
    rows, freqs, block, _ = inverse_own.shape
    for r in range(2 * rows):
        cols = slice(r * block, (r + 1) * block)
        inverse = inverse_own if r < rows else inverse_got
        total = own[:, cols] + got1[:, cols].astype(jnp.float32)
        total += got2[:, cols].astype(jnp.float32) + got3[:, cols].astype(jnp.float32)
        load[:, cols] = total
        solved = nt_dot(
            total.astype(jnp.bfloat16), inverse[r % rows].reshape(freqs * block, block)
        )
        initial[:, cols] = diagonal(solved, freqs).astype(jnp.bfloat16)


def step_kernel(
    active, place, near, far, previous, load, transfer_own, transfer_got, inverse_own, inverse_got,
    out, state,
):
    rows, nonzero, freqs, block, _ = transfer_own.shape

    @pl.when(active[0] == 1)
    def _():
        for r in range(2 * rows):
            state[r] = near[:, r * block:(r + 1) * block]
            state[2 * rows + r] = far[:, r * block:(r + 1) * block]
        for r in range(2 * rows):
            cols = slice(r * block, (r + 1) * block)
            transfer, inverse = (
                (transfer_own, inverse_own) if r < rows else (transfer_got, inverse_got)
            )
            picked = jnp.concatenate([state[place[r * nonzero + k]] for k in range(nonzero)], axis=1)
            matrix = jnp.concatenate(
                [transfer[r % rows, k].reshape(freqs * block, block) for k in range(nonzero)], axis=1
            )
            summed = (load[:, cols] + diagonal(nt_dot(picked, matrix), freqs)).astype(jnp.bfloat16)
            solved = nt_dot(summed, inverse[r % rows].reshape(freqs * block, block))
            out[:, cols] = diagonal(solved, freqs).astype(jnp.bfloat16)

    @pl.when(active[0] != 1)
    def _():
        out[...] = previous[...]


def moved(value, distance, offset):
    bays, secs = lax.axis_size("bay"), lax.axis_size("sec")
    route = [
        (b * secs + s, (b + distance) % bays * secs + (s ^ offset))
        for b in range(bays)
        for s in range(secs)
    ]
    return lax.ppermute(value, ("bay", "sec"), route)


def hop(value, source, offset):
    bays, secs = lax.axis_size("bay"), lax.axis_size("sec")
    route = [
        (source * secs + s, (source + 1) % bays * secs + (s ^ offset)) for s in range(secs)
    ]
    return lax.ppermute(value, ("bay", "sec"), route)


def per_device(edge_load, interior_load, coupling, block_cols, transfer, local_inverse):
    _, freqs, cases, width = edge_load.shape
    _, rows, nonzero, _, block, _ = transfer.shape
    inner = interior_load.shape[-1]
    half = freqs // 2
    lines = half * cases
    sec = lax.axis_index("sec")
    position = lax.axis_index("bay")
    bays = lax.axis_size("bay")
    edge = edge_load.reshape(freqs * cases, width)
    interior = interior_load.reshape(freqs * cases, inner)
    sec_word = sec.astype(jnp.int32).reshape(1)
    params = pltpu.CompilerParams(vmem_limit_bytes=24 * MIB)
    bf16, f32 = jnp.bfloat16, jnp.float32
    wide = (lines, 2 * width)

    piece2, piece3 = pl.pallas_call(
        far_kernel,
        out_shape=[jax.ShapeDtypeStruct(wide, bf16)] * 2,
        in_specs=[SMEM, VMEM, ANY],
        out_specs=[VMEM] * 2,
        scratch_shapes=[pltpu.VMEM((2, inner, width), bf16), pltpu.SemaphoreType.DMA((2,))],
        compiler_params=params,
        name="far",
    )(sec_word, interior, coupling[0])
    got2, got3 = moved(piece2, 0, 2), moved(piece3, 0, 3)

    matrices = (rows, nonzero, half, block, block)
    inverses = (rows, half, block, block)
    piece1, own, transfer_own, transfer_out, inverse_own, inverse_out = pl.pallas_call(
        near_kernel,
        out_shape=[
            jax.ShapeDtypeStruct(wide, bf16),
            jax.ShapeDtypeStruct(wide, f32),
            pltpu.VMEM(matrices, bf16),
            pltpu.VMEM(matrices, bf16),
            pltpu.VMEM(inverses, bf16),
            pltpu.VMEM(inverses, bf16),
        ],
        in_specs=[SMEM, VMEM, VMEM, ANY, ANY, ANY],
        out_specs=[VMEM] * 6,
        scratch_shapes=[pltpu.VMEM((2, inner, width), bf16), pltpu.SemaphoreType.DMA((6,))],
        compiler_params=params,
        name="near",
    )(sec_word, interior, edge, coupling[0], transfer[0], local_inverse[0])
    got1 = moved(piece1, 0, 1)
    inverse_got = moved(inverse_out, 0, 1)
    transfer_got = moved(transfer_out, 0, 1)

    cols = block_cols[0]
    cols = jnp.concatenate([cols, moved(cols, 0, 1)], axis=0)
    place = ((cols // rows) ^ sec) * rows + cols % rows
    place = place.reshape(-1).astype(jnp.int32)

    load, state = pl.pallas_call(
        initial_kernel,
        out_shape=[jax.ShapeDtypeStruct(wide, f32), jax.ShapeDtypeStruct(wide, bf16)],
        in_specs=[VMEM] * 6,
        out_specs=[VMEM] * 2,
        compiler_params=params,
        name="initial",
    )(own, got1, got2, got3, inverse_own, inverse_got)

    for step in range(bays):
        source = (step - 1) % bays
        near, far = hop(state, source, 0), hop(state, source, 2)
        active = (position == step).astype(jnp.int32).reshape(1)
        state = pl.pallas_call(
            step_kernel,
            out_shape=jax.ShapeDtypeStruct(wide, bf16),
            in_specs=[SMEM, SMEM] + [VMEM] * 8,
            out_specs=VMEM,
            scratch_shapes=[pltpu.VMEM((4 * rows, lines, block), bf16)],
            compiler_params=params,
            name="step",
        )(active, place, near, far, state, load, transfer_own, transfer_got, inverse_own, inverse_got)

    kept, sent = state[:, :width], state[:, width:]
    got = moved(sent, 0, 1)
    odd = (sec & 1) == 1
    low, high = jnp.where(odd, got, kept), jnp.where(odd, kept, got)
    return jnp.concatenate([low, high], axis=0).reshape(1, freqs, cases, width)


def solution(mesh):
    in_specs = (
        P(("groups", "bay"), None, None, "sec"),
        P(("groups", "bay"), None, None, "sec"),
        P(("groups", "bay"), "sec", None),
        P(("groups", "bay"), "sec", None),
        P(("groups", "bay"), "sec", None, None, None, None),
        P(("groups", "bay"), "sec", None, None, None),
    )
    out_specs = P(("groups", "bay"), None, None, "sec")
    return jax.shard_map(
        per_device, mesh=mesh, in_specs=in_specs, out_specs=out_specs, check_vma=False
    )
```

```python
import functools

import jax
import jax.numpy as jnp
from jax import lax
from jax.experimental import pallas as pl
from jax.experimental.pallas import tpu as pltpu
from jax.sharding import PartitionSpec as P

VMEM = pl.BlockSpec(memory_space=pltpu.VMEM)
SMEM = pl.BlockSpec(memory_space=pltpu.SMEM)
ANY = pl.BlockSpec(memory_space=pl.ANY)
MIB = 1 << 20


def nt_dot(left, right):
    return lax.dot_general(left, right, (((1,), (1,)), ((), ())), preferred_element_type=jnp.float32)


def diagonal(product, freqs):
    rows, cols = product.shape[0] // freqs, product.shape[1] // freqs
    return jnp.concatenate(
        [product[f * rows:(f + 1) * rows, f * cols:(f + 1) * cols] for f in range(freqs)], axis=0
    )


def by_parity(odd, rows):
    half = rows.shape[0] // 2
    return jnp.where(odd, rows[half:], rows[:half]), jnp.where(odd, rows[:half], rows[half:])


def columns_of(coupling, owner, width):
    return coupling.at[:, pl.ds(pl.multiple_of(owner * width, width), width)]


def far_kernel(sec_ref, interior, coupling, piece2, piece3, held, sems):
    sec = sec_ref[0]
    width = held.shape[-1]
    copies = [
        pltpu.make_async_copy(columns_of(coupling, sec ^ d, width), held.at[n], sems.at[n])
        for n, d in enumerate((2, 3))
    ]
    for copy in copies:
        copy.start()
    pieces = {2: piece2, 3: piece3}
    for n, d in enumerate((2, 3)):
        copies[n].wait()
        part = -jnp.dot(interior[...], held[n], preferred_element_type=jnp.float32)
        first, second = by_parity(((sec ^ d) & 1) == 1, part)
        pieces[d][:, :width] = first.astype(jnp.bfloat16)
        pieces[d ^ 1][:, width:] = second.astype(jnp.bfloat16)


def near_kernel(
    sec_ref, interior, edge, coupling, transfer, inverse, after,
    piece1, own, transfer_out, inverse_out, held, sems,
):
    sec = sec_ref[0]
    width = held.shape[-1]
    odd = (sec & 1) == 1
    half = transfer.shape[2] // 2
    other = half - (sec & 1) * half
    copies = [
        pltpu.make_async_copy(columns_of(coupling, sec ^ d, width), held.at[n], sems.at[n])
        for n, d in enumerate((1, 0))
    ]
    moves = [
        pltpu.make_async_copy(inverse.at[:, pl.ds(other, half)], inverse_out, sems.at[2]),
        pltpu.make_async_copy(transfer.at[:, :, pl.ds(other, half)], transfer_out, sems.at[3]),
    ]
    for copy in copies + moves:
        copy.start()
    copies[0].wait()
    part = -jnp.dot(interior[...], held[0], preferred_element_type=jnp.float32)
    first, second = by_parity(jnp.logical_not(odd), part)
    piece1[:, :width] = first.astype(jnp.bfloat16)
    own[:, width:] = second
    copies[1].wait()
    part = edge[...].astype(jnp.float32) - jnp.dot(
        interior[...], held[1], preferred_element_type=jnp.float32
    )
    first, second = by_parity(odd, part)
    own[:, :width] = first
    piece1[:, width:] = second.astype(jnp.bfloat16)
    for move in moves:
        move.wait()


def inverse_kernel(sec_ref, inverse, got, held, sems):
    rows, half = got.shape[:2]
    mine = (sec_ref[0] & 1) * half
    copies = [
        pltpu.make_async_copy(inverse.at[:, pl.ds(mine, half)], held.at[pl.ds(0, rows)], sems.at[0]),
        pltpu.make_async_copy(got, held.at[pl.ds(rows, rows)], sems.at[1]),
    ]
    for copy in copies:
        copy.start()
    for copy in copies:
        copy.wait()


def transfer_kernel(sec_ref, transfer, got, after, held, sems):
    rows, _, half = got.shape[:3]
    mine = (sec_ref[0] & 1) * half
    copies = [
        pltpu.make_async_copy(
            transfer.at[:, :, pl.ds(mine, half)], held.at[pl.ds(0, rows)], sems.at[0]
        ),
        pltpu.make_async_copy(got, held.at[pl.ds(rows, rows)], sems.at[1]),
    ]
    for copy in copies:
        copy.start()
    for copy in copies:
        copy.wait()


def initial_kernel(own, got1, got2, got3, inverse, load, initial):
    rows, freqs, block, _ = inverse.shape
    for r in range(rows):
        cols = slice(r * block, (r + 1) * block)
        total = own[:, cols] + got1[:, cols].astype(jnp.float32)
        total += got2[:, cols].astype(jnp.float32) + got3[:, cols].astype(jnp.float32)
        load[:, cols] = total
        solved = nt_dot(total.astype(jnp.bfloat16), inverse[r].reshape(freqs * block, block))
        initial[:, cols] = diagonal(solved, freqs).astype(jnp.bfloat16)


def step_kernel(step, bay_ref, sec_ref, cols_own, cols_got, near, far, previous, load, transfer, inverse, out, state):
    rows, nonzero, freqs, block, _ = transfer.shape
    part = rows // 2
    sec = sec_ref[0]

    @pl.when(bay_ref[0] == step)
    def _():
        for n in range(2):
            source = (near, far)[n]
            for r in range(rows):
                home = (sec ^ (2 * n + r // part)) * part + r % part
                state[home] = source[:, r * block:(r + 1) * block]
        for r in range(rows):
            cols = slice(r * block, (r + 1) * block)
            ids = cols_own if r < part else cols_got
            picked = jnp.concatenate([state[ids[r % part, k]] for k in range(nonzero)], axis=1)
            matrix = jnp.concatenate(
                [transfer[r, k].reshape(freqs * block, block) for k in range(nonzero)], axis=1
            )
            summed = (load[:, cols] + diagonal(nt_dot(picked, matrix), freqs)).astype(jnp.bfloat16)
            solved = nt_dot(summed, inverse[r].reshape(freqs * block, block))
            out[:, cols] = diagonal(solved, freqs).astype(jnp.bfloat16)

    @pl.when(bay_ref[0] != step)
    def _():
        out[...] = previous[...]


def finish_kernel(sec_ref, state, got, out):
    lines, width = got.shape
    odd = (sec_ref[0] & 1) == 1

    @pl.when(odd)
    def _():
        out[:lines] = got[...]
        out[lines:] = state[:, :width]

    @pl.when(jnp.logical_not(odd))
    def _():
        out[:lines] = state[:, :width]
        out[lines:] = got[...]


def moved(value, distance, offset):
    bays, secs = lax.axis_size("bay"), lax.axis_size("sec")
    route = [
        (b * secs + s, (b + distance) % bays * secs + (s ^ offset))
        for b in range(bays)
        for s in range(secs)
    ]
    return lax.ppermute(value, ("bay", "sec"), route)


def hop(value, source, offset):
    bays, secs = lax.axis_size("bay"), lax.axis_size("sec")
    route = [
        (source * secs + s, (source + 1) % bays * secs + (s ^ offset)) for s in range(secs)
    ]
    return lax.ppermute(value, ("bay", "sec"), route)


def per_device(edge_load, interior_load, coupling, block_cols, transfer, local_inverse):
    _, freqs, cases, width = edge_load.shape
    _, rows, nonzero, _, block, _ = transfer.shape
    inner = interior_load.shape[-1]
    half = freqs // 2
    lines = half * cases
    sec = lax.axis_index("sec").astype(jnp.int32)
    position = lax.axis_index("bay")
    bays = lax.axis_size("bay")
    edge = edge_load.reshape(freqs * cases, width)
    interior = interior_load.reshape(freqs * cases, inner)
    sec_word = sec.reshape(1)
    alone = pltpu.CompilerParams(vmem_limit_bytes=60 * MIB)
    beside = pltpu.CompilerParams(vmem_limit_bytes=48 * MIB)
    small = pltpu.CompilerParams(vmem_limit_bytes=12 * MIB)
    bf16, f32 = jnp.bfloat16, jnp.float32
    wide = (lines, 2 * width)
    matrices = (rows, nonzero, half, block, block)
    inverses = (rows, half, block, block)
    held_block = pltpu.VMEM((2, inner, width), bf16)

    piece2, piece3 = pl.pallas_call(
        far_kernel,
        out_shape=[jax.ShapeDtypeStruct(wide, bf16)] * 2,
        in_specs=[SMEM, VMEM, ANY],
        out_specs=[VMEM] * 2,
        scratch_shapes=[held_block, pltpu.SemaphoreType.DMA((2,))],
        compiler_params=alone,
        name="far",
    )(sec_word, interior, coupling[0])
    got2, got3 = moved(piece2, 0, 2), moved(piece3, 0, 3)
    cols_own = block_cols[0]
    cols_got = moved(cols_own, 0, 1)

    piece1, own, transfer_out, inverse_out = pl.pallas_call(
        near_kernel,
        out_shape=[
            jax.ShapeDtypeStruct(wide, bf16),
            jax.ShapeDtypeStruct(wide, f32),
            jax.ShapeDtypeStruct(matrices, bf16),
            jax.ShapeDtypeStruct(inverses, bf16),
        ],
        in_specs=[SMEM, VMEM, VMEM, ANY, ANY, ANY, ANY],
        out_specs=[VMEM, VMEM, VMEM, VMEM],
        scratch_shapes=[held_block, pltpu.SemaphoreType.DMA((4,))],
        compiler_params=alone,
        name="near",
    )(sec_word, interior, edge, coupling[0], transfer[0], local_inverse[0], piece2)
    got1 = moved(piece1, 0, 1)
    inverse_got = moved(inverse_out, 0, 1)
    transfer_got = moved(transfer_out, 0, 1)

    inverse = pl.pallas_call(
        inverse_kernel,
        out_shape=pltpu.VMEM((2 * rows, half, block, block), bf16),
        in_specs=[SMEM, ANY, ANY],
        out_specs=VMEM,
        scratch_shapes=[pltpu.SemaphoreType.DMA((2,))],
        compiler_params=alone,
        name="inverse",
    )(sec_word, local_inverse[0], inverse_got)

    load, state = pl.pallas_call(
        initial_kernel,
        out_shape=[jax.ShapeDtypeStruct(wide, f32), jax.ShapeDtypeStruct(wide, bf16)],
        in_specs=[VMEM] * 5,
        out_specs=[VMEM] * 2,
        compiler_params=small,
        name="initial",
    )(own, got1, got2, got3, inverse)

    matrix = pl.pallas_call(
        transfer_kernel,
        out_shape=pltpu.VMEM((2 * rows, nonzero, half, block, block), bf16),
        in_specs=[SMEM, ANY, ANY, ANY],
        out_specs=VMEM,
        scratch_shapes=[pltpu.SemaphoreType.DMA((2,))],
        compiler_params=beside,
        name="transfer",
    )(sec_word, transfer[0], transfer_got, state)

    bay_word = position.astype(jnp.int32).reshape(1)
    for step in range(bays):
        source = (step - 1) % bays
        near, far = hop(state, source, 0), hop(state, source, 2)
        state = pl.pallas_call(
            functools.partial(step_kernel, step),
            out_shape=jax.ShapeDtypeStruct(wide, bf16),
            in_specs=[SMEM] * 4 + [VMEM] * 6,
            out_specs=VMEM,
            scratch_shapes=[pltpu.VMEM((4 * rows, lines, block), bf16)],
            compiler_params=small,
            name="step",
        )(bay_word, sec_word, cols_own, cols_got, near, far, state, load, matrix, inverse)

    got = moved(state[:, width:], 0, 1)
    result = pl.pallas_call(
        finish_kernel,
        out_shape=jax.ShapeDtypeStruct((2 * lines, width), bf16),
        in_specs=[SMEM, VMEM, VMEM],
        out_specs=VMEM,
        compiler_params=small,
        name="finish",
    )(sec_word, state, got)
    return result.reshape(1, freqs, cases, width)


def solution(mesh):
    in_specs = (
        P(("groups", "bay"), None, None, "sec"),
        P(("groups", "bay"), None, None, "sec"),
        P(("groups", "bay"), "sec", None),
        P(("groups", "bay"), "sec", None),
        P(("groups", "bay"), "sec", None, None, None, None),
        P(("groups", "bay"), "sec", None, None, None),
    )
    out_specs = P(("groups", "bay"), None, None, "sec")
    return jax.shard_map(
        per_device, mesh=mesh, in_specs=in_specs, out_specs=out_specs, check_vma=False
    )
```

```python
import functools

import jax
import jax.numpy as jnp
from jax import lax
from jax.experimental import pallas as pl
from jax.experimental.pallas import tpu as pltpu
from jax.sharding import PartitionSpec as P

VMEM = pl.BlockSpec(memory_space=pltpu.VMEM)
SMEM = pl.BlockSpec(memory_space=pltpu.SMEM)
ANY = pl.BlockSpec(memory_space=pl.ANY)
MIB = 1 << 20


def nt_dot(left, right):
    return lax.dot_general(left, right, (((1,), (1,)), ((), ())), preferred_element_type=jnp.float32)


def diagonal(product, freqs):
    rows, cols = product.shape[0] // freqs, product.shape[1] // freqs
    return jnp.concatenate(
        [product[f * rows:(f + 1) * rows, f * cols:(f + 1) * cols] for f in range(freqs)], axis=0
    )


def by_parity(odd, rows):
    half = rows.shape[0] // 2
    return jnp.where(odd, rows[half:], rows[:half]), jnp.where(odd, rows[:half], rows[half:])


def columns_of(coupling, owner, width):
    return coupling.at[:, pl.ds(pl.multiple_of(owner * width, width), width)]


def force_kernel(
    sec_ref, bay_ref, cols, interior, edge, coupling, inverse,
    piece1, piece2, piece3, own, inverse_own, inverse_out, loads, held, sems,
):
    sec = sec_ref[0]
    width = held.shape[-1]
    half = inverse.shape[1] // 2
    mine = (sec & 1) * half
    loads_in = pltpu.make_async_copy(interior, loads.at[0], sems.at[4])
    edge_in = pltpu.make_async_copy(edge, loads.at[1], sems.at[5])
    loads_in.start()
    order = (2, 3, 1, 0)
    copies = [
        pltpu.make_async_copy(columns_of(coupling, sec ^ d, width), held.at[n], sems.at[n])
        for n, d in enumerate(order)
    ]
    for copy in copies:
        copy.start()
    edge_in.start()
    moves = [
        pltpu.make_async_copy(inverse.at[:, pl.ds(half - mine, half)], inverse_out, sems.at[6]),
        pltpu.make_async_copy(inverse.at[:, pl.ds(mine, half)], inverse_own, sems.at[7]),
    ]
    for move in moves:
        move.start()
    loads_in.wait()
    pieces = (own, piece1, piece2, piece3)
    for n, d in enumerate(order):
        copies[n].wait()
        part = -jnp.dot(loads[0], held[n], preferred_element_type=jnp.float32)
        if d == 0:
            edge_in.wait()
            part += loads[1].astype(jnp.float32)
        first, second = by_parity(((sec ^ d) & 1) == 1, part)
        pieces[d][:, :width] = first.astype(pieces[d].dtype)
        pieces[d ^ 1][:, width:] = second.astype(pieces[d ^ 1].dtype)
    for move in moves:
        move.wait()


def transfer_kernel(sec_ref, transfer, after, transfer_out, transfer_own, sems):
    half = transfer_own.shape[2]
    mine = (sec_ref[0] & 1) * half
    copies = [
        pltpu.make_async_copy(transfer.at[:, :, pl.ds(half - mine, half)], transfer_out, sems.at[0]),
        pltpu.make_async_copy(transfer.at[:, :, pl.ds(mine, half)], transfer_own, sems.at[1]),
    ]
    for copy in copies:
        copy.start()
    for copy in copies:
        copy.wait()


def initial_kernel(own, got1, got2, got3, inverse_own, inverse_got, after, load, initial):
    part, freqs, block, _ = inverse_own.shape
    for r in range(2 * part):
        inverse = inverse_own if r < part else inverse_got
        cols = slice(r * block, (r + 1) * block)
        total = own[:, cols] + got1[:, cols].astype(jnp.float32)
        total += got2[:, cols].astype(jnp.float32) + got3[:, cols].astype(jnp.float32)
        load[:, cols] = total
        solved = nt_dot(total.astype(jnp.bfloat16), inverse[r % part].reshape(freqs * block, block))
        initial[:, cols] = diagonal(solved, freqs).astype(jnp.bfloat16)


def step_kernel(
    step, bay_ref, sec_ref, cols_own, cols_got, near, far, previous, load,
    transfer_own, transfer_got, inverse_own, inverse_got, out, state,
):
    part, nonzero, freqs, block, _ = transfer_own.shape
    rows = 2 * part
    sec = sec_ref[0]

    @pl.when(bay_ref[0] == step)
    def _():
        for n in range(2):
            source = (near, far)[n]
            for r in range(rows):
                home = (sec ^ (2 * n + r // part)) * part + r % part
                state[home] = source[:, r * block:(r + 1) * block]
        for r in range(rows):
            cols = slice(r * block, (r + 1) * block)
            own = r < part
            ids = cols_own if own else cols_got
            transfer = transfer_own if own else transfer_got
            inverse = inverse_own if own else inverse_got
            picked = jnp.concatenate([state[ids[r % part, k]] for k in range(nonzero)], axis=1)
            matrix = jnp.concatenate(
                [transfer[r % part, k].reshape(freqs * block, block) for k in range(nonzero)], axis=1
            )
            summed = (load[:, cols] + diagonal(nt_dot(picked, matrix), freqs)).astype(jnp.bfloat16)
            solved = nt_dot(summed, inverse[r % part].reshape(freqs * block, block))
            out[:, cols] = diagonal(solved, freqs).astype(jnp.bfloat16)

    @pl.when(bay_ref[0] != step)
    def _():
        out[...] = previous[...]


def finish_kernel(sec_ref, state, got, out):
    lines, width = got.shape
    odd = (sec_ref[0] & 1) == 1

    @pl.when(odd)
    def _():
        out[:lines] = got[...]
        out[lines:] = state[:, :width]

    @pl.when(jnp.logical_not(odd))
    def _():
        out[:lines] = state[:, :width]
        out[lines:] = got[...]


def in_hbm(value):
    return pltpu.with_memory_space_constraint(value, pltpu.HBM)


def moved(value, distance, offset):
    bays, secs = lax.axis_size("bay"), lax.axis_size("sec")
    route = [
        (b * secs + s, (b + distance) % bays * secs + (s ^ offset))
        for b in range(bays)
        for s in range(secs)
    ]
    return lax.ppermute(value, ("bay", "sec"), route)


def hop(value, source, offset):
    return moved(value, 1, offset)


def per_device(edge_load, interior_load, coupling, block_cols, transfer, local_inverse):
    _, freqs, cases, width = edge_load.shape
    _, rows, nonzero, _, block, _ = transfer.shape
    inner = interior_load.shape[-1]
    half = freqs // 2
    lines = half * cases
    sec = lax.axis_index("sec").astype(jnp.int32)
    position = lax.axis_index("bay")
    bays = lax.axis_size("bay")
    edge = edge_load.reshape(freqs * cases, width)
    interior = interior_load.reshape(freqs * cases, inner)
    sec_word = sec.reshape(1)
    bay_word = position.astype(jnp.int32).reshape(1)
    params = pltpu.CompilerParams(vmem_limit_bytes=16 * MIB)
    bf16, f32 = jnp.bfloat16, jnp.float32
    wide = (lines, 2 * width)
    matrices = (rows, nonzero, half, block, block)
    inverses = (rows, half, block, block)

    cols_own = block_cols[0]
    piece1, piece2, piece3, own, inverse_own, inverse_out = pl.pallas_call(
        force_kernel,
        out_shape=[jax.ShapeDtypeStruct(wide, bf16)] * 3
        + [jax.ShapeDtypeStruct(wide, f32)]
        + [pltpu.VMEM(inverses, bf16)] * 2,
        in_specs=[SMEM, SMEM, SMEM, ANY, ANY, ANY, ANY],
        out_specs=[VMEM] * 6,
        scratch_shapes=[
            pltpu.VMEM((2, 2 * lines, inner), bf16),
            pltpu.VMEM((4, inner, width), bf16),
            pltpu.SemaphoreType.DMA((8,)),
        ],
        compiler_params=params,
        name="force",
    )(sec_word, bay_word, cols_own, in_hbm(interior), in_hbm(edge), in_hbm(coupling[0]), in_hbm(local_inverse[0]))
    got2, got3, got1 = moved(piece2, 0, 2), moved(piece3, 0, 3), moved(piece1, 0, 1)
    inverse_got = moved(inverse_out, 0, 1)
    cols_got = moved(cols_own, 0, 1)

    transfer_out, transfer_own = pl.pallas_call(
        transfer_kernel,
        out_shape=[pltpu.VMEM(matrices, bf16)] * 2,
        in_specs=[SMEM, ANY, ANY],
        out_specs=[VMEM] * 2,
        scratch_shapes=[pltpu.SemaphoreType.DMA((2,))],
        compiler_params=params,
        name="transfer",
    )(sec_word, in_hbm(transfer[0]), piece2)
    transfer_got = moved(transfer_out, 0, 1)

    load, state = pl.pallas_call(
        initial_kernel,
        out_shape=[jax.ShapeDtypeStruct(wide, f32), jax.ShapeDtypeStruct(wide, bf16)],
        in_specs=[VMEM] * 6 + [ANY],
        out_specs=[VMEM] * 2,
        compiler_params=params,
        name="initial",
    )(own, got1, got2, got3, inverse_own, inverse_got, transfer_own)

    for step in range(bays):
        source = (step - 1) % bays
        near, far = hop(state, source, 0), hop(state, source, 2)
        state = pl.pallas_call(
            functools.partial(step_kernel, step),
            out_shape=jax.ShapeDtypeStruct(wide, bf16),
            in_specs=[SMEM] * 4 + [VMEM] * 8,
            out_specs=VMEM,
            scratch_shapes=[pltpu.VMEM((4 * rows, lines, block), bf16)],
            compiler_params=params,
            name="step",
        )(bay_word, sec_word, cols_own, cols_got, near, far, state, load,
          transfer_own, transfer_got, inverse_own, inverse_got)

    got = moved(state[:, width:], 0, 1)
    result = pl.pallas_call(
        finish_kernel,
        out_shape=jax.ShapeDtypeStruct((2 * lines, width), bf16),
        in_specs=[SMEM, VMEM, VMEM],
        out_specs=VMEM,
        compiler_params=params,
        name="finish",
    )(sec_word, state, got)
    return result.reshape(1, freqs, cases, width)


def solution(mesh):
    in_specs = (
        P(("groups", "bay"), None, None, "sec"),
        P(("groups", "bay"), None, None, "sec"),
        P(("groups", "bay"), "sec", None),
        P(("groups", "bay"), "sec", None),
        P(("groups", "bay"), "sec", None, None, None, None),
        P(("groups", "bay"), "sec", None, None, None),
    )
    out_specs = P(("groups", "bay"), None, None, "sec")
    return jax.shard_map(
        per_device, mesh=mesh, in_specs=in_specs, out_specs=out_specs, check_vma=False
    )
```

```python
import functools

import jax
import jax.numpy as jnp
from jax import lax
from jax.experimental import pallas as pl
from jax.experimental.pallas import tpu as pltpu
from jax.sharding import PartitionSpec as P

VMEM = pl.BlockSpec(memory_space=pltpu.VMEM)
SMEM = pl.BlockSpec(memory_space=pltpu.SMEM)
ANY = pl.BlockSpec(memory_space=pl.ANY)
MIB = 1 << 20


def nt_dot(left, right):
    return lax.dot_general(left, right, (((1,), (1,)), ((), ())), preferred_element_type=jnp.float32)


def diagonal(product, freqs):
    rows, cols = product.shape[0] // freqs, product.shape[1] // freqs
    return jnp.concatenate(
        [product[f * rows:(f + 1) * rows, f * cols:(f + 1) * cols] for f in range(freqs)], axis=0
    )


def by_parity(odd, rows):
    half = rows.shape[0] // 2
    return jnp.where(odd, rows[half:], rows[:half]), jnp.where(odd, rows[:half], rows[half:])


def columns_of(coupling, owner, width):
    return coupling.at[:, pl.ds(pl.multiple_of(owner * width, width), width)]


def force_kernel(
    interior, edge, coupling, inverse,
    piece1, piece2, piece3, own, inverse_own, inverse_out, loads, held, sems,
):
    sec = lax.axis_index("sec")
    width = held.shape[-1]
    half = inverse.shape[1] // 2
    mine = (sec & 1) * half
    loads_in = pltpu.make_async_copy(interior, loads.at[0], sems.at[4])
    edge_in = pltpu.make_async_copy(edge, loads.at[1], sems.at[5])
    loads_in.start()
    order = (2, 3, 1, 0)
    copies = [
        pltpu.make_async_copy(columns_of(coupling, sec ^ d, width), held.at[n], sems.at[n])
        for n, d in enumerate(order)
    ]
    for copy in copies:
        copy.start()
    edge_in.start()
    moves = [
        pltpu.make_async_copy(inverse.at[:, pl.ds(half - mine, half)], inverse_out, sems.at[6]),
        pltpu.make_async_copy(inverse.at[:, pl.ds(mine, half)], inverse_own, sems.at[7]),
    ]
    for move in moves:
        move.start()
    loads_in.wait()
    pieces = (own, piece1, piece2, piece3)
    for n, d in enumerate(order):
        copies[n].wait()
        part = -jnp.dot(loads[0], held[n], preferred_element_type=jnp.float32)
        if d == 0:
            edge_in.wait()
            part += loads[1].astype(jnp.float32)
        first, second = by_parity(((sec ^ d) & 1) == 1, part)
        pieces[d][:, :width] = first.astype(pieces[d].dtype)
        pieces[d ^ 1][:, width:] = second.astype(pieces[d ^ 1].dtype)
    for move in moves:
        move.wait()


def transfer_kernel(transfer, after, transfer_out, transfer_own, sems):
    half = transfer_own.shape[2]
    mine = (lax.axis_index("sec") & 1) * half
    copies = [
        pltpu.make_async_copy(transfer.at[:, :, pl.ds(half - mine, half)], transfer_out, sems.at[0]),
        pltpu.make_async_copy(transfer.at[:, :, pl.ds(mine, half)], transfer_own, sems.at[1]),
    ]
    for copy in copies:
        copy.start()
    for copy in copies:
        copy.wait()


def initial_kernel(own, got1, got2, got3, inverse_own, inverse_got, after, load, initial, passed):
    part, freqs, block, _ = inverse_own.shape
    for r in range(2 * part):
        inverse = inverse_own if r < part else inverse_got
        cols = slice(r * block, (r + 1) * block)
        total = own[:, cols] + got1[:, cols].astype(jnp.float32)
        total += got2[:, cols].astype(jnp.float32) + got3[:, cols].astype(jnp.float32)
        load[:, cols] = total
        solved = nt_dot(total.astype(jnp.bfloat16), inverse[r % part].reshape(freqs * block, block))
        initial[:, cols] = diagonal(solved, freqs).astype(jnp.bfloat16)


def step_kernel(
    step, cols_own, cols_got, near, far, previous, load,
    transfer_own, transfer_got, inverse_own, inverse_got, out, state,
):
    part, nonzero, freqs, block, _ = transfer_own.shape
    rows = 2 * part
    sec = lax.axis_index("sec")
    bay = lax.axis_index("bay")

    @pl.when(bay == step)
    def _():
        for n in range(2):
            source = (near, far)[n]
            for r in range(rows):
                home = (sec ^ (2 * n + r // part)) * part + r % part
                state[home] = source[:, r * block:(r + 1) * block]
        for r in range(rows):
            cols = slice(r * block, (r + 1) * block)
            own = r < part
            ids = cols_own if own else cols_got
            transfer = transfer_own if own else transfer_got
            inverse = inverse_own if own else inverse_got
            picked = jnp.concatenate([state[ids[r % part, 0, k]] for k in range(nonzero)], axis=1)
            matrix = jnp.concatenate(
                [transfer[r % part, k].reshape(freqs * block, block) for k in range(nonzero)], axis=1
            )
            summed = (load[:, cols] + diagonal(nt_dot(picked, matrix), freqs)).astype(jnp.bfloat16)
            solved = nt_dot(summed, inverse[r % part].reshape(freqs * block, block))
            out[:, cols] = diagonal(solved, freqs).astype(jnp.bfloat16)

    @pl.when(bay != step)
    def _():
        out[...] = previous[...]


def finish_kernel(state, got, out):
    lines, width = got.shape
    odd = (lax.axis_index("sec") & 1) == 1

    @pl.when(odd)
    def _():
        out[:lines] = got[...]
        out[lines:] = state[:, :width]

    @pl.when(jnp.logical_not(odd))
    def _():
        out[:lines] = state[:, :width]
        out[lines:] = got[...]


def in_hbm(value):
    return pltpu.with_memory_space_constraint(value, pltpu.HBM)


def moved(value, distance, offset):
    bays, secs = lax.axis_size("bay"), lax.axis_size("sec")
    route = [
        (b * secs + s, (b + distance) % bays * secs + (s ^ offset))
        for b in range(bays)
        for s in range(secs)
    ]
    return lax.ppermute(value, ("bay", "sec"), route)


def hop(value, source, offset):
    return moved(value, 1, offset)


def per_device(edge_load, interior_load, coupling, block_cols, transfer, local_inverse):
    _, freqs, cases, width = edge_load.shape
    _, rows, nonzero, _, block, _ = transfer.shape
    inner = interior_load.shape[-1]
    half = freqs // 2
    lines = half * cases
    bays = lax.axis_size("bay")
    edge = edge_load.reshape(freqs * cases, width)
    interior = interior_load.reshape(freqs * cases, inner)
    params = pltpu.CompilerParams(vmem_limit_bytes=16 * MIB)
    bf16, f32 = jnp.bfloat16, jnp.float32
    wide = (lines, 2 * width)
    matrices = (rows, nonzero, half, block, block)
    inverses = (rows, half, block, block)

    cols_own = jnp.transpose(block_cols, (1, 0, 2))
    piece1, piece2, piece3, own, inverse_own, inverse_out = pl.pallas_call(
        force_kernel,
        out_shape=[jax.ShapeDtypeStruct(wide, bf16)] * 3
        + [jax.ShapeDtypeStruct(wide, f32)]
        + [pltpu.VMEM(inverses, bf16)] * 2,
        in_specs=[ANY] * 4,
        out_specs=[VMEM] * 6,
        scratch_shapes=[
            pltpu.VMEM((2, 2 * lines, inner), bf16),
            pltpu.VMEM((4, inner, width), bf16),
            pltpu.SemaphoreType.DMA((8,)),
        ],
        compiler_params=params,
        name="force",
    )(in_hbm(interior), in_hbm(edge), in_hbm(coupling[0]), in_hbm(local_inverse[0]))
    got2, got3, got1 = moved(piece2, 0, 2), moved(piece3, 0, 3), moved(piece1, 0, 1)
    inverse_got = moved(inverse_out, 0, 1)
    cols_got = moved(cols_own, 0, 1)

    transfer_out, transfer_own = pl.pallas_call(
        transfer_kernel,
        out_shape=[pltpu.VMEM(matrices, bf16)] * 2,
        in_specs=[ANY, ANY],
        out_specs=[VMEM] * 2,
        scratch_shapes=[pltpu.SemaphoreType.DMA((2,))],
        compiler_params=params,
        name="transfer",
    )(in_hbm(transfer[0]), got1)
    load, state, transfer_out = pl.pallas_call(
        initial_kernel,
        out_shape=[
            jax.ShapeDtypeStruct(wide, f32),
            jax.ShapeDtypeStruct(wide, bf16),
            pltpu.VMEM(matrices, bf16),
        ],
        in_specs=[VMEM] * 6 + [ANY],
        out_specs=[VMEM, VMEM, ANY],
        input_output_aliases={6: 2},
        compiler_params=params,
        name="initial",
    )(own, got1, got2, got3, inverse_own, inverse_got, transfer_out)
    transfer_got = moved(transfer_out, 0, 1)

    for step in range(bays):
        source = (step - 1) % bays
        near, far = hop(state, source, 0), hop(state, source, 2)
        state = pl.pallas_call(
            functools.partial(step_kernel, step),
            out_shape=jax.ShapeDtypeStruct(wide, bf16),
            in_specs=[SMEM] * 2 + [VMEM] * 8,
            out_specs=VMEM,
            scratch_shapes=[pltpu.VMEM((4 * rows, lines, block), bf16)],
            compiler_params=params,
            name="step",
        )(cols_own, cols_got, near, far, state, load,
          transfer_own, transfer_got, inverse_own, inverse_got)

    got = moved(state[:, width:], 0, 1)
    result = pl.pallas_call(
        finish_kernel,
        out_shape=jax.ShapeDtypeStruct((2 * lines, width), bf16),
        in_specs=[VMEM, VMEM],
        out_specs=VMEM,
        compiler_params=params,
        name="finish",
    )(state, got)
    return result.reshape(1, freqs, cases, width)


def solution(mesh):
    in_specs = (
        P(("groups", "bay"), None, None, "sec"),
        P(("groups", "bay"), None, None, "sec"),
        P(("groups", "bay"), "sec", None),
        P(("groups", "bay"), "sec", None),
        P(("groups", "bay"), "sec", None, None, None, None),
        P(("groups", "bay"), "sec", None, None, None),
    )
    out_specs = P(("groups", "bay"), None, None, "sec")
    return jax.shard_map(
        per_device, mesh=mesh, in_specs=in_specs, out_specs=out_specs, check_vma=False
    )
```

```python
import functools

import jax
import jax.numpy as jnp
from jax import lax
from jax.experimental import pallas as pl
from jax.experimental.pallas import tpu as pltpu
from jax.sharding import PartitionSpec as P

VMEM = pl.BlockSpec(memory_space=pltpu.VMEM)
SMEM = pl.BlockSpec(memory_space=pltpu.SMEM)
ANY = pl.BlockSpec(memory_space=pl.ANY)
MIB = 1 << 20


def nt_dot(left, right):
    return lax.dot_general(left, right, (((1,), (1,)), ((), ())), preferred_element_type=jnp.float32)


def nn_dot(left, right):
    return jnp.dot(left, right, preferred_element_type=jnp.float32)


def diagonal(product, freqs):
    rows, cols = product.shape[0] // freqs, product.shape[1] // freqs
    return jnp.concatenate(
        [product[f * rows:(f + 1) * rows, f * cols:(f + 1) * cols] for f in range(freqs)], axis=0
    )


def by_parity(odd, rows):
    half = rows.shape[0] // 2
    return jnp.where(odd, rows[half:], rows[:half]), jnp.where(odd, rows[:half], rows[half:])


def columns_of(coupling, owner, width):
    return coupling.at[:, pl.ds(pl.multiple_of(owner * width, width), width)]


def force_kernel(
    interior, edge, coupling, inverse,
    piece1, piece2, piece3, own, inverse_own, inverse_out, loads, held, sems,
):
    sec = lax.axis_index("sec")
    width = held.shape[-1]
    half = inverse.shape[1] // 2
    mine = (sec & 1) * half
    loads_in = pltpu.make_async_copy(interior, loads.at[0], sems.at[4])
    edge_in = pltpu.make_async_copy(edge, loads.at[1], sems.at[5])
    loads_in.start()
    order = (2, 3, 1, 0)
    copies = [
        pltpu.make_async_copy(columns_of(coupling, sec ^ d, width), held.at[n], sems.at[n])
        for n, d in enumerate(order)
    ]
    for copy in copies:
        copy.start()
    edge_in.start()
    moves = [
        pltpu.make_async_copy(inverse.at[:, pl.ds(half - mine, half)], inverse_out, sems.at[6]),
        pltpu.make_async_copy(inverse.at[:, pl.ds(mine, half)], inverse_own, sems.at[7]),
    ]
    for move in moves:
        move.start()
    loads_in.wait()
    pieces = (own, piece1, piece2, piece3)
    for n, d in enumerate(order):
        copies[n].wait()
        part = -jnp.dot(loads[0], held[n], preferred_element_type=jnp.float32)
        if d == 0:
            edge_in.wait()
            part += loads[1].astype(jnp.float32)
        first, second = by_parity(((sec ^ d) & 1) == 1, part)
        pieces[d][:, :width] = first.astype(pieces[d].dtype)
        pieces[d ^ 1][:, width:] = second.astype(pieces[d ^ 1].dtype)
    for move in moves:
        move.wait()


def transfer_kernel(
    transfer, inverse_own, inverse_got, after, transfer_out, transfer_own, turned, raw, sems,
):
    rows, nonzero, half = transfer_own.shape[:3]
    mine = (lax.axis_index("sec") & 1) * half
    targets = [(transfer_out, half - mine), (transfer_own, mine)]
    copies = [
        pltpu.make_async_copy(
            transfer.at[r, :, pl.ds(first, half)], raw.at[n * rows + r], sems.at[n * rows + r]
        )
        for n, (_, first) in enumerate(targets)
        for r in range(rows)
    ]
    for copy in copies:
        copy.start()
    for r in range(rows):
        for f in range(half):
            turned[r, f] = inverse_own[r, f].T
            turned[rows + r, f] = inverse_got[r, f].T
    for n, (target, _) in enumerate(targets):
        for r in range(rows):
            copies[n * rows + r].wait()
            for k in range(nonzero):
                for f in range(half):
                    target[r, k, f] = raw[n * rows + r, k, f].T


def initial_kernel(own, got1, got2, got3, inverse_own, inverse_got, after, load, initial, passed):
    part, freqs, block, _ = inverse_own.shape
    for r in range(2 * part):
        inverse = inverse_own if r < part else inverse_got
        cols = slice(r * block, (r + 1) * block)
        total = own[:, cols] + got1[:, cols].astype(jnp.float32)
        total += got2[:, cols].astype(jnp.float32) + got3[:, cols].astype(jnp.float32)
        load[:, cols] = total
        solved = nt_dot(total.astype(jnp.bfloat16), inverse[r % part].reshape(freqs * block, block))
        initial[:, cols] = diagonal(solved, freqs).astype(jnp.bfloat16)


def step_kernel(
    step, near, far, previous, load,
    transfer_own, transfer_got, inverse, cols_own, cols_got, out, state, ids, sems,
):
    part, nonzero, freqs, block, _ = transfer_own.shape
    rows = 2 * part
    sec = lax.axis_index("sec")
    bay = lax.axis_index("bay")

    @pl.when(bay == step)
    def _():
        copies = [
            pltpu.make_async_copy(cols, ids.at[n], sems.at[n]) for n, cols in enumerate((cols_own, cols_got))
        ]
        for copy in copies:
            copy.start()
        for n in range(2):
            source = (near, far)[n]
            for r in range(rows):
                home = (sec ^ (2 * n + r // part)) * part + r % part
                state[home] = source[:, r * block:(r + 1) * block]
        for copy in copies:
            copy.wait()
        for r in range(rows):
            cols = slice(r * block, (r + 1) * block)
            transfer = transfer_own if r < part else transfer_got
            picked = jnp.concatenate([state[ids[r // part, r % part, 0, k]] for k in range(nonzero)], axis=1)
            matrix = jnp.concatenate(
                [jnp.concatenate([transfer[r % part, k, f] for f in range(freqs)], axis=1) for k in range(nonzero)],
                axis=0,
            )
            summed = (load[:, cols] + diagonal(nn_dot(picked, matrix), freqs)).astype(jnp.bfloat16)
            solved = nn_dot(summed, jnp.concatenate([inverse[r, f] for f in range(freqs)], axis=1))
            out[:, cols] = diagonal(solved, freqs).astype(jnp.bfloat16)

    @pl.when(bay != step)
    def _():
        out[...] = previous[...]


def finish_kernel(state, got, out):
    lines, width = got.shape
    odd = (lax.axis_index("sec") & 1) == 1

    @pl.when(odd)
    def _():
        out[:lines] = got[...]
        out[lines:] = state[:, :width]

    @pl.when(jnp.logical_not(odd))
    def _():
        out[:lines] = state[:, :width]
        out[lines:] = got[...]


def in_hbm(value):
    return pltpu.with_memory_space_constraint(value, pltpu.HBM)


def moved(value, distance, offset):
    bays, secs = lax.axis_size("bay"), lax.axis_size("sec")
    route = [
        (b * secs + s, (b + distance) % bays * secs + (s ^ offset))
        for b in range(bays)
        for s in range(secs)
    ]
    return lax.ppermute(value, ("bay", "sec"), route)


def hop(value, source, offset):
    return moved(value, 1, offset)


def per_device(edge_load, interior_load, coupling, block_cols, transfer, local_inverse):
    _, freqs, cases, width = edge_load.shape
    _, rows, nonzero, _, block, _ = transfer.shape
    inner = interior_load.shape[-1]
    half = freqs // 2
    lines = half * cases
    bays = lax.axis_size("bay")
    edge = edge_load.reshape(freqs * cases, width)
    interior = interior_load.reshape(freqs * cases, inner)
    params = pltpu.CompilerParams(vmem_limit_bytes=20 * MIB)
    bf16, f32 = jnp.bfloat16, jnp.float32
    wide = (lines, 2 * width)
    matrices = (rows, nonzero, half, block, block)
    inverses = (rows, half, block, block)

    cols_own = jnp.transpose(block_cols, (1, 0, 2))
    piece1, piece2, piece3, own, inverse_own, inverse_out = pl.pallas_call(
        force_kernel,
        out_shape=[jax.ShapeDtypeStruct(wide, bf16)] * 3
        + [jax.ShapeDtypeStruct(wide, f32)]
        + [pltpu.VMEM(inverses, bf16)] * 2,
        in_specs=[ANY] * 4,
        out_specs=[VMEM] * 6,
        scratch_shapes=[
            pltpu.VMEM((2, 2 * lines, inner), bf16),
            pltpu.VMEM((4, inner, width), bf16),
            pltpu.SemaphoreType.DMA((8,)),
        ],
        compiler_params=params,
        name="force",
    )(in_hbm(interior), in_hbm(edge), in_hbm(coupling[0]), in_hbm(local_inverse[0]))
    got2, got3, got1 = moved(piece2, 0, 2), moved(piece3, 0, 3), moved(piece1, 0, 1)
    inverse_got = moved(inverse_out, 0, 1)
    cols_got = moved(cols_own, 0, 1)

    transfer_out, transfer_own, turned = pl.pallas_call(
        transfer_kernel,
        out_shape=[pltpu.VMEM(matrices, bf16)] * 2
        + [pltpu.VMEM((2 * rows,) + inverses[1:], bf16)],
        in_specs=[ANY, VMEM, VMEM, ANY],
        out_specs=[VMEM] * 3,
        scratch_shapes=[
            pltpu.VMEM((2 * rows,) + matrices[1:], bf16),
            pltpu.SemaphoreType.DMA((2 * rows,)),
        ],
        compiler_params=params,
        name="transfer",
    )(in_hbm(transfer[0]), inverse_own, inverse_got, got1)
    load, state, transfer_out = pl.pallas_call(
        initial_kernel,
        out_shape=[
            jax.ShapeDtypeStruct(wide, f32),
            jax.ShapeDtypeStruct(wide, bf16),
            pltpu.VMEM(matrices, bf16),
        ],
        in_specs=[VMEM] * 6 + [ANY],
        out_specs=[VMEM, VMEM, ANY],
        input_output_aliases={6: 2},
        compiler_params=params,
        name="initial",
    )(own, got1, got2, got3, inverse_own, inverse_got, transfer_out)
    transfer_got = moved(transfer_out, 0, 1)

    for step in range(bays):
        source = (step - 1) % bays
        near, far = hop(state, source, 0), hop(state, source, 2)
        state = pl.pallas_call(
            functools.partial(step_kernel, step),
            out_shape=jax.ShapeDtypeStruct(wide, bf16),
            in_specs=[VMEM] * 9,
            out_specs=VMEM,
            scratch_shapes=[
                pltpu.VMEM((4 * rows, lines, block), bf16),
                pltpu.SMEM((2,) + cols_own.shape, jnp.int32),
                pltpu.SemaphoreType.DMA((2,)),
            ],
            compiler_params=params,
            name="step",
        )(near, far, state, load, transfer_own, transfer_got, turned, cols_own, cols_got)

    got = moved(state[:, width:], 0, 1)
    result = pl.pallas_call(
        finish_kernel,
        out_shape=jax.ShapeDtypeStruct((2 * lines, width), bf16),
        in_specs=[VMEM, VMEM],
        out_specs=VMEM,
        compiler_params=params,
        name="finish",
    )(state, got)
    return result.reshape(1, freqs, cases, width)


def solution(mesh):
    in_specs = (
        P(("groups", "bay"), None, None, "sec"),
        P(("groups", "bay"), None, None, "sec"),
        P(("groups", "bay"), "sec", None),
        P(("groups", "bay"), "sec", None),
        P(("groups", "bay"), "sec", None, None, None, None),
        P(("groups", "bay"), "sec", None, None, None),
    )
    out_specs = P(("groups", "bay"), None, None, "sec")
    return jax.shard_map(
        per_device, mesh=mesh, in_specs=in_specs, out_specs=out_specs, check_vma=False
    )
```

```python
import functools

import jax
import jax.numpy as jnp
from jax import lax
from jax.experimental import pallas as pl
from jax.experimental.pallas import tpu as pltpu
from jax.sharding import PartitionSpec as P

VMEM = pl.BlockSpec(memory_space=pltpu.VMEM)
SMEM = pl.BlockSpec(memory_space=pltpu.SMEM)
ANY = pl.BlockSpec(memory_space=pl.ANY)
MIB = 1 << 20


def nt_dot(left, right):
    return lax.dot_general(left, right, (((1,), (1,)), ((), ())), preferred_element_type=jnp.float32)


def nn_dot(left, right):
    return jnp.dot(left, right, preferred_element_type=jnp.float32)


def diagonal(product, freqs):
    rows, cols = product.shape[0] // freqs, product.shape[1] // freqs
    return jnp.concatenate(
        [product[f * rows:(f + 1) * rows, f * cols:(f + 1) * cols] for f in range(freqs)], axis=0
    )


def by_parity(odd, rows):
    half = rows.shape[0] // 2
    return jnp.where(odd, rows[half:], rows[:half]), jnp.where(odd, rows[:half], rows[half:])


def columns_of(coupling, owner, width):
    return coupling.at[:, pl.ds(pl.multiple_of(owner * width, width), width)]


def force_kernel(
    interior, edge, coupling, inverse,
    piece1, piece2, piece3, own, inverse_own, inverse_out, loads, held, sems,
):
    sec = lax.axis_index("sec")
    width = held.shape[-1]
    half = inverse.shape[1] // 2
    mine = (sec & 1) * half
    loads_in = pltpu.make_async_copy(interior, loads.at[0], sems.at[4])
    edge_in = pltpu.make_async_copy(edge, loads.at[1], sems.at[5])
    loads_in.start()
    order = (2, 3, 1, 0)
    copies = [
        pltpu.make_async_copy(columns_of(coupling, sec ^ d, width), held.at[n], sems.at[n])
        for n, d in enumerate(order)
    ]
    for copy in copies:
        copy.start()
    edge_in.start()
    moves = [
        pltpu.make_async_copy(inverse.at[:, pl.ds(half - mine, half)], inverse_out, sems.at[6]),
        pltpu.make_async_copy(inverse.at[:, pl.ds(mine, half)], inverse_own, sems.at[7]),
    ]
    for move in moves:
        move.start()
    loads_in.wait()
    pieces = (own, piece1, piece2, piece3)
    for n, d in enumerate(order):
        copies[n].wait()
        part = -jnp.dot(loads[0], held[n], preferred_element_type=jnp.float32)
        if d == 0:
            edge_in.wait()
            part += loads[1].astype(jnp.float32)
        first, second = by_parity(((sec ^ d) & 1) == 1, part)
        pieces[d][:, :width] = first.astype(pieces[d].dtype)
        pieces[d ^ 1][:, width:] = second.astype(pieces[d ^ 1].dtype)
    for move in moves:
        move.wait()


def transfer_kernel(
    transfer, inverse_own, inverse_got, after, transfer_out, transfer_own, turned, raw, sems,
):
    rows, nonzero, half = transfer_own.shape[:3]
    mine = (lax.axis_index("sec") & 1) * half
    targets = [(transfer_out, half - mine), (transfer_own, mine)]
    copies = [
        pltpu.make_async_copy(
            transfer.at[r, :, pl.ds(first, half)], raw.at[n * rows + r], sems.at[n * rows + r]
        )
        for n, (_, first) in enumerate(targets)
        for r in range(rows)
    ]
    for copy in copies:
        copy.start()
    for r in range(rows):
        for f in range(half):
            turned[r, f] = inverse_own[r, f].T
            turned[rows + r, f] = inverse_got[r, f].T
    for n, (target, _) in enumerate(targets):
        for r in range(rows):
            copies[n * rows + r].wait()
            for k in range(nonzero):
                for f in range(half):
                    target[r, k, f] = raw[n * rows + r, k, f].T


def initial_kernel(own, got1, got2, got3, inverse_own, inverse_got, after, load, initial, passed):
    part, freqs, block, _ = inverse_own.shape
    for r in range(2 * part):
        inverse = inverse_own if r < part else inverse_got
        cols = slice(r * block, (r + 1) * block)
        total = own[:, cols] + got1[:, cols].astype(jnp.float32)
        total += got2[:, cols].astype(jnp.float32) + got3[:, cols].astype(jnp.float32)
        load[:, cols] = total
        solved = nt_dot(total.astype(jnp.bfloat16), inverse[r % part].reshape(freqs * block, block))
        initial[:, cols] = diagonal(solved, freqs).astype(jnp.bfloat16)


def step_kernel(
    step, near, far, previous, load,
    transfer_own, transfer_got, inverse, cols_own, cols_got, out, state, ids, sems,
):
    part, nonzero, freqs, block, _ = transfer_own.shape
    rows = 2 * part
    sec = lax.axis_index("sec")
    bay = lax.axis_index("bay")

    @pl.when(bay == step)
    def _():
        copies = [
            pltpu.make_async_copy(cols, ids.at[n], sems.at[n]) for n, cols in enumerate((cols_own, cols_got))
        ]
        for copy in copies:
            copy.start()
        for n in range(2):
            source = (near, far)[n]
            for r in range(rows):
                home = (sec ^ (2 * n + r // part)) * part + r % part
                state[home] = source[:, r * block:(r + 1) * block]
        for copy in copies:
            copy.wait()
        for r in range(rows):
            cols = slice(r * block, (r + 1) * block)
            transfer = transfer_own if r < part else transfer_got
            picked = jnp.concatenate([state[ids[r // part, r % part, 0, k]] for k in range(nonzero)], axis=1)
            matrix = jnp.concatenate(
                [jnp.concatenate([transfer[r % part, k, f] for f in range(freqs)], axis=1) for k in range(nonzero)],
                axis=0,
            )
            summed = (load[:, cols] + diagonal(nn_dot(picked, matrix), freqs)).astype(jnp.bfloat16)
            solved = nn_dot(summed, jnp.concatenate([inverse[r, f] for f in range(freqs)], axis=1))
            out[:, cols] = diagonal(solved, freqs).astype(jnp.bfloat16)

    @pl.when(bay != step)
    def _():
        out[...] = previous[...]


def finish_kernel(state, got, out):
    lines, width = got.shape
    odd = (lax.axis_index("sec") & 1) == 1

    @pl.when(odd)
    def _():
        out[:lines] = got[...]
        out[lines:] = state[:, :width]

    @pl.when(jnp.logical_not(odd))
    def _():
        out[:lines] = state[:, :width]
        out[lines:] = got[...]


def in_hbm(value):
    return pltpu.with_memory_space_constraint(value, pltpu.HBM)


def moved(value, distance, offset):
    bays, secs = lax.axis_size("bay"), lax.axis_size("sec")
    route = [
        (b * secs + s, (b + distance) % bays * secs + (s ^ offset))
        for b in range(bays)
        for s in range(secs)
    ]
    return lax.ppermute(value, ("bay", "sec"), route)


def hop(value, source, offset):
    bays, secs = lax.axis_size("bay"), lax.axis_size("sec")
    target = (source + 1) % bays
    cycle = list(range(bays))
    if bays > 3 and target > 0:
        cycle = [source, target, source + 2]
        if target == bays - 1:
            cycle = [source, target, 0, 1]
        elif target == 1:
            cycle = [0, 1, 3, 2]
    goes = {b: cycle[(n + 1) % len(cycle)] for n, b in enumerate(cycle)}
    route = [
        (b * secs + s, goes[b] * secs + (s ^ offset) if b in goes else b * secs + (s ^ 1))
        for b in range(bays)
        for s in range(secs)
    ]
    return lax.ppermute(value, ("bay", "sec"), route)


def per_device(edge_load, interior_load, coupling, block_cols, transfer, local_inverse):
    _, freqs, cases, width = edge_load.shape
    _, rows, nonzero, _, block, _ = transfer.shape
    inner = interior_load.shape[-1]
    half = freqs // 2
    lines = half * cases
    bays = lax.axis_size("bay")
    edge = edge_load.reshape(freqs * cases, width)
    interior = interior_load.reshape(freqs * cases, inner)
    params = pltpu.CompilerParams(vmem_limit_bytes=20 * MIB)
    bf16, f32 = jnp.bfloat16, jnp.float32
    wide = (lines, 2 * width)
    matrices = (rows, nonzero, half, block, block)
    inverses = (rows, half, block, block)

    cols_own = jnp.transpose(block_cols, (1, 0, 2))
    piece1, piece2, piece3, own, inverse_own, inverse_out = pl.pallas_call(
        force_kernel,
        out_shape=[jax.ShapeDtypeStruct(wide, bf16)] * 3
        + [jax.ShapeDtypeStruct(wide, f32)]
        + [pltpu.VMEM(inverses, bf16)] * 2,
        in_specs=[ANY] * 4,
        out_specs=[VMEM] * 6,
        scratch_shapes=[
            pltpu.VMEM((2, 2 * lines, inner), bf16),
            pltpu.VMEM((4, inner, width), bf16),
            pltpu.SemaphoreType.DMA((8,)),
        ],
        compiler_params=params,
        name="force",
    )(in_hbm(interior), in_hbm(edge), in_hbm(coupling[0]), in_hbm(local_inverse[0]))
    got2, got3, got1 = moved(piece2, 0, 2), moved(piece3, 0, 3), moved(piece1, 0, 1)
    inverse_got = moved(inverse_out, 0, 1)
    cols_got = moved(cols_own, 0, 1)

    transfer_out, transfer_own, turned = pl.pallas_call(
        transfer_kernel,
        out_shape=[pltpu.VMEM(matrices, bf16)] * 2
        + [pltpu.VMEM((2 * rows,) + inverses[1:], bf16)],
        in_specs=[ANY, VMEM, VMEM, ANY],
        out_specs=[VMEM] * 3,
        scratch_shapes=[
            pltpu.VMEM((2 * rows,) + matrices[1:], bf16),
            pltpu.SemaphoreType.DMA((2 * rows,)),
        ],
        compiler_params=params,
        name="transfer",
    )(in_hbm(transfer[0]), inverse_own, inverse_got, got1)
    load, state, transfer_out = pl.pallas_call(
        initial_kernel,
        out_shape=[
            jax.ShapeDtypeStruct(wide, f32),
            jax.ShapeDtypeStruct(wide, bf16),
            pltpu.VMEM(matrices, bf16),
        ],
        in_specs=[VMEM] * 6 + [ANY],
        out_specs=[VMEM, VMEM, ANY],
        input_output_aliases={6: 2},
        compiler_params=params,
        name="initial",
    )(own, got1, got2, got3, inverse_own, inverse_got, transfer_out)
    transfer_got = moved(transfer_out, 0, 1)

    for step in range(bays):
        source = (step - 1) % bays
        near, far = hop(state, source, 0), hop(state, source, 2)
        state = pl.pallas_call(
            functools.partial(step_kernel, step),
            out_shape=jax.ShapeDtypeStruct(wide, bf16),
            in_specs=[VMEM] * 9,
            out_specs=VMEM,
            scratch_shapes=[
                pltpu.VMEM((4 * rows, lines, block), bf16),
                pltpu.SMEM((2,) + cols_own.shape, jnp.int32),
                pltpu.SemaphoreType.DMA((2,)),
            ],
            compiler_params=params,
            name="step",
        )(near, far, state, load, transfer_own, transfer_got, turned, cols_own, cols_got)

    got = moved(state[:, width:], 0, 1)
    result = pl.pallas_call(
        finish_kernel,
        out_shape=jax.ShapeDtypeStruct((2 * lines, width), bf16),
        in_specs=[VMEM, VMEM],
        out_specs=VMEM,
        compiler_params=params,
        name="finish",
    )(state, got)
    return result.reshape(1, freqs, cases, width)


def solution(mesh):
    in_specs = (
        P(("groups", "bay"), None, None, "sec"),
        P(("groups", "bay"), None, None, "sec"),
        P(("groups", "bay"), "sec", None),
        P(("groups", "bay"), "sec", None),
        P(("groups", "bay"), "sec", None, None, None, None),
        P(("groups", "bay"), "sec", None, None, None),
    )
    out_specs = P(("groups", "bay"), None, None, "sec")
    return jax.shard_map(
        per_device, mesh=mesh, in_specs=in_specs, out_specs=out_specs, check_vma=False
    )
```

```python
import functools

import jax
import jax.numpy as jnp
from jax import lax
from jax.experimental import pallas as pl
from jax.experimental.pallas import tpu as pltpu
from jax.sharding import PartitionSpec as P

VMEM = pl.BlockSpec(memory_space=pltpu.VMEM)
SMEM = pl.BlockSpec(memory_space=pltpu.SMEM)
ANY = pl.BlockSpec(memory_space=pl.ANY)
MIB = 1 << 20


def nt_dot(left, right):
    return lax.dot_general(left, right, (((1,), (1,)), ((), ())), preferred_element_type=jnp.float32)


def nn_dot(left, right):
    return jnp.dot(left, right, preferred_element_type=jnp.float32)


def diagonal(product, freqs):
    rows, cols = product.shape[0] // freqs, product.shape[1] // freqs
    return jnp.concatenate(
        [product[f * rows:(f + 1) * rows, f * cols:(f + 1) * cols] for f in range(freqs)], axis=0
    )


def by_parity(odd, rows):
    half = rows.shape[0] // 2
    return jnp.where(odd, rows[half:], rows[:half]), jnp.where(odd, rows[:half], rows[half:])


def columns_of(coupling, owner, width):
    return coupling.at[:, pl.ds(pl.multiple_of(owner * width, width), width)]


def force_kernel(
    interior, edge, coupling, inverse,
    piece1, piece2, piece3, own, inverse_own, inverse_out, loads, held, sems,
):
    sec = lax.axis_index("sec")
    width = held.shape[-1]
    half = inverse.shape[1] // 2
    mine = (sec & 1) * half
    loads_in = pltpu.make_async_copy(interior, loads.at[0], sems.at[4])
    edge_in = pltpu.make_async_copy(edge, loads.at[1], sems.at[5])
    loads_in.start()
    order = (2, 3, 1, 0)
    copies = [
        pltpu.make_async_copy(columns_of(coupling, sec ^ d, width), held.at[n], sems.at[n])
        for n, d in enumerate(order)
    ]
    for copy in copies:
        copy.start()
    edge_in.start()
    moves = [
        pltpu.make_async_copy(inverse.at[:, pl.ds(half - mine, half)], inverse_out, sems.at[6]),
        pltpu.make_async_copy(inverse.at[:, pl.ds(mine, half)], inverse_own, sems.at[7]),
    ]
    for move in moves:
        move.start()
    loads_in.wait()
    pieces = (own, piece1, piece2, piece3)
    for n, d in enumerate(order):
        copies[n].wait()
        part = -jnp.dot(loads[0], held[n], preferred_element_type=jnp.float32)
        if d == 0:
            edge_in.wait()
            part += loads[1].astype(jnp.float32)
        first, second = by_parity(((sec ^ d) & 1) == 1, part)
        pieces[d][:, :width] = first.astype(pieces[d].dtype)
        pieces[d ^ 1][:, width:] = second.astype(pieces[d ^ 1].dtype)
    for move in moves:
        move.wait()


def transfer_kernel(
    transfer, inverse_own, inverse_got, after, transfer_out, transfer_own, turned, raw, sems,
):
    rows, nonzero, half = transfer_own.shape[:3]
    mine = (lax.axis_index("sec") & 1) * half
    targets = [(transfer_out, half - mine), (transfer_own, mine)]
    copies = [
        pltpu.make_async_copy(
            transfer.at[r, :, pl.ds(first, half)], raw.at[n * rows + r], sems.at[n * rows + r]
        )
        for n, (_, first) in enumerate(targets)
        for r in range(rows)
    ]
    for copy in copies:
        copy.start()
    for r in range(rows):
        for f in range(half):
            turned[r, f] = inverse_own[r, f].T
            turned[rows + r, f] = inverse_got[r, f].T
    for n, (target, _) in enumerate(targets):
        for r in range(rows):
            copies[n * rows + r].wait()
            for k in range(nonzero):
                for f in range(half):
                    target[r, k, f] = raw[n * rows + r, k, f].T


def initial_kernel(own, got1, got2, got3, inverse_own, inverse_got, after, load, initial, passed):
    part, freqs, block, _ = inverse_own.shape
    for r in range(2 * part):
        inverse = inverse_own if r < part else inverse_got
        cols = slice(r * block, (r + 1) * block)
        total = own[:, cols] + got1[:, cols].astype(jnp.float32)
        total += got2[:, cols].astype(jnp.float32) + got3[:, cols].astype(jnp.float32)
        load[:, cols] = total
        solved = nt_dot(total.astype(jnp.bfloat16), inverse[r % part].reshape(freqs * block, block))
        initial[:, cols] = diagonal(solved, freqs).astype(jnp.bfloat16)


def step_kernel(
    step, far, near, previous, load,
    transfer_own, transfer_got, inverse, cols_own, cols_got, out, state, ids, sems,
):
    part, nonzero, freqs, block, _ = transfer_own.shape
    rows = 2 * part
    sec = lax.axis_index("sec")
    bay = lax.axis_index("bay")

    @pl.when(bay == step)
    def _():
        copies = [
            pltpu.make_async_copy(cols, ids.at[n], sems.at[n]) for n, cols in enumerate((cols_own, cols_got))
        ]
        for copy in copies:
            copy.start()
        for n in range(2):
            source = (near, far)[n]
            for r in range(rows):
                home = (sec ^ (2 * n + r // part)) * part + r % part
                state[home] = source[:, r * block:(r + 1) * block]
        for copy in copies:
            copy.wait()
        for r in range(rows):
            cols = slice(r * block, (r + 1) * block)
            transfer = transfer_own if r < part else transfer_got
            picked = jnp.concatenate([state[ids[r // part, r % part, 0, k]] for k in range(nonzero)], axis=1)
            matrix = jnp.concatenate(
                [jnp.concatenate([transfer[r % part, k, f] for f in range(freqs)], axis=1) for k in range(nonzero)],
                axis=0,
            )
            summed = (load[:, cols] + diagonal(nn_dot(picked, matrix), freqs)).astype(jnp.bfloat16)
            solved = nn_dot(summed, jnp.concatenate([inverse[r, f] for f in range(freqs)], axis=1))
            out[:, cols] = diagonal(solved, freqs).astype(jnp.bfloat16)

    @pl.when(bay != step)
    def _():
        out[...] = previous[...]


def finish_kernel(state, got, out):
    lines, width = got.shape
    odd = (lax.axis_index("sec") & 1) == 1

    @pl.when(odd)
    def _():
        out[:lines] = got[...]
        out[lines:] = state[:, :width]

    @pl.when(jnp.logical_not(odd))
    def _():
        out[:lines] = state[:, :width]
        out[lines:] = got[...]


def in_hbm(value):
    return pltpu.with_memory_space_constraint(value, pltpu.HBM)


def moved(value, distance, offset):
    bays, secs = lax.axis_size("bay"), lax.axis_size("sec")
    route = [
        (b * secs + s, (b + distance) % bays * secs + (s ^ offset))
        for b in range(bays)
        for s in range(secs)
    ]
    return lax.ppermute(value, ("bay", "sec"), route)


def hop(value, source, offset):
    bays, secs = lax.axis_size("bay"), lax.axis_size("sec")
    target = (source + 1) % bays
    cycle = list(range(bays))
    if bays > 3 and target == 1:
        cycle = [0, 1, 3, 2]
    elif bays > 3 and target > 1:
        cycle = [source, target, target + 1 if target + 1 < bays else source - 1]
    goes = {b: cycle[(n + 1) % len(cycle)] for n, b in enumerate(cycle)}
    route = [
        (b * secs + s, goes[b] * secs + (s ^ offset) if b in goes else b * secs + (s ^ 1))
        for b in range(bays)
        for s in range(secs)
    ]
    return lax.ppermute(value, ("bay", "sec"), route)


def per_device(edge_load, interior_load, coupling, block_cols, transfer, local_inverse):
    _, freqs, cases, width = edge_load.shape
    _, rows, nonzero, _, block, _ = transfer.shape
    inner = interior_load.shape[-1]
    half = freqs // 2
    lines = half * cases
    bays = lax.axis_size("bay")
    edge = edge_load.reshape(freqs * cases, width)
    interior = interior_load.reshape(freqs * cases, inner)
    params = pltpu.CompilerParams(vmem_limit_bytes=20 * MIB)
    bf16, f32 = jnp.bfloat16, jnp.float32
    wide = (lines, 2 * width)
    matrices = (rows, nonzero, half, block, block)
    inverses = (rows, half, block, block)

    cols_own = jnp.transpose(block_cols, (1, 0, 2))
    piece1, piece2, piece3, own, inverse_own, inverse_out = pl.pallas_call(
        force_kernel,
        out_shape=[jax.ShapeDtypeStruct(wide, bf16)] * 3
        + [jax.ShapeDtypeStruct(wide, f32)]
        + [pltpu.VMEM(inverses, bf16)] * 2,
        in_specs=[ANY] * 4,
        out_specs=[VMEM] * 6,
        scratch_shapes=[
            pltpu.VMEM((2, 2 * lines, inner), bf16),
            pltpu.VMEM((4, inner, width), bf16),
            pltpu.SemaphoreType.DMA((8,)),
        ],
        compiler_params=params,
        name="force",
    )(in_hbm(interior), in_hbm(edge), in_hbm(coupling[0]), in_hbm(local_inverse[0]))
    got2, got3, got1 = moved(piece2, 0, 2), moved(piece3, 0, 3), moved(piece1, 0, 1)
    inverse_got = moved(inverse_out, 0, 1)
    cols_got = moved(cols_own, 0, 1)

    transfer_out, transfer_own, turned = pl.pallas_call(
        transfer_kernel,
        out_shape=[pltpu.VMEM(matrices, bf16)] * 2
        + [pltpu.VMEM((2 * rows,) + inverses[1:], bf16)],
        in_specs=[ANY, VMEM, VMEM, ANY],
        out_specs=[VMEM] * 3,
        scratch_shapes=[
            pltpu.VMEM((2 * rows,) + matrices[1:], bf16),
            pltpu.SemaphoreType.DMA((2 * rows,)),
        ],
        compiler_params=params,
        name="transfer",
    )(in_hbm(transfer[0]), inverse_own, inverse_got, got1)
    load, state, transfer_out = pl.pallas_call(
        initial_kernel,
        out_shape=[
            jax.ShapeDtypeStruct(wide, f32),
            jax.ShapeDtypeStruct(wide, bf16),
            pltpu.VMEM(matrices, bf16),
        ],
        in_specs=[VMEM] * 6 + [ANY],
        out_specs=[VMEM, VMEM, ANY],
        input_output_aliases={6: 2},
        compiler_params=params,
        name="initial",
    )(own, got1, got2, got3, inverse_own, inverse_got, transfer_out)
    transfer_got = moved(transfer_out, 0, 1)

    for step in range(bays):
        source = (step - 1) % bays
        far = hop(state, source, 2)
        near = hop(state, source, 0)
        state = pl.pallas_call(
            functools.partial(step_kernel, step),
            out_shape=jax.ShapeDtypeStruct(wide, bf16),
            in_specs=[VMEM] * 9,
            out_specs=VMEM,
            scratch_shapes=[
                pltpu.VMEM((4 * rows, lines, block), bf16),
                pltpu.SMEM((2,) + cols_own.shape, jnp.int32),
                pltpu.SemaphoreType.DMA((2,)),
            ],
            compiler_params=params,
            name="step",
        )(far, near, state, load, transfer_own, transfer_got, turned, cols_own, cols_got)

    got = moved(state[:, width:], 0, 1)
    result = pl.pallas_call(
        finish_kernel,
        out_shape=jax.ShapeDtypeStruct((2 * lines, width), bf16),
        in_specs=[VMEM, VMEM],
        out_specs=VMEM,
        compiler_params=params,
        name="finish",
    )(state, got)
    return result.reshape(1, freqs, cases, width)


def solution(mesh):
    in_specs = (
        P(("groups", "bay"), None, None, "sec"),
        P(("groups", "bay"), None, None, "sec"),
        P(("groups", "bay"), "sec", None),
        P(("groups", "bay"), "sec", None),
        P(("groups", "bay"), "sec", None, None, None, None),
        P(("groups", "bay"), "sec", None, None, None),
    )
    out_specs = P(("groups", "bay"), None, None, "sec")
    return jax.shard_map(
        per_device, mesh=mesh, in_specs=in_specs, out_specs=out_specs, check_vma=False
    )
```

```python
import functools

import jax
import jax.numpy as jnp
from jax import lax
from jax.experimental import pallas as pl
from jax.experimental.pallas import tpu as pltpu
from jax.sharding import PartitionSpec as P

VMEM = pl.BlockSpec(memory_space=pltpu.VMEM)
SMEM = pl.BlockSpec(memory_space=pltpu.SMEM)
ANY = pl.BlockSpec(memory_space=pl.ANY)
MIB = 1 << 20


def nt_dot(left, right):
    return lax.dot_general(left, right, (((1,), (1,)), ((), ())), preferred_element_type=jnp.float32)


def nn_dot(left, right):
    return jnp.dot(left, right, preferred_element_type=jnp.float32)


def diagonal(product, freqs):
    rows, cols = product.shape[0] // freqs, product.shape[1] // freqs
    return jnp.concatenate(
        [product[f * rows:(f + 1) * rows, f * cols:(f + 1) * cols] for f in range(freqs)], axis=0
    )


def by_parity(odd, rows):
    half = rows.shape[0] // 2
    return jnp.where(odd, rows[half:], rows[:half]), jnp.where(odd, rows[:half], rows[half:])


def columns_of(coupling, owner, width):
    return coupling.at[:, pl.ds(pl.multiple_of(owner * width, width), width)]


def force_kernel(
    interior, edge, coupling, inverse,
    piece1, piece2, piece3, own, inverse_own, inverse_out, loads, held, sems,
):
    sec = lax.axis_index("sec")
    width = held.shape[-1]
    half = inverse.shape[1] // 2
    mine = (sec & 1) * half
    loads_in = pltpu.make_async_copy(interior, loads.at[0], sems.at[4])
    edge_in = pltpu.make_async_copy(edge, loads.at[1], sems.at[5])
    loads_in.start()
    order = (2, 3, 1, 0)
    copies = [
        pltpu.make_async_copy(columns_of(coupling, sec ^ d, width), held.at[n], sems.at[n])
        for n, d in enumerate(order)
    ]
    for copy in copies:
        copy.start()
    edge_in.start()
    moves = [
        pltpu.make_async_copy(inverse.at[:, pl.ds(half - mine, half)], inverse_out, sems.at[6]),
        pltpu.make_async_copy(inverse.at[:, pl.ds(mine, half)], inverse_own, sems.at[7]),
    ]
    for move in moves:
        move.start()
    loads_in.wait()
    pieces = (own, piece1, piece2, piece3)
    for n, d in enumerate(order):
        copies[n].wait()
        part = -jnp.dot(loads[0], held[n], preferred_element_type=jnp.float32)
        if d == 0:
            edge_in.wait()
            part += loads[1].astype(jnp.float32)
        first, second = by_parity(((sec ^ d) & 1) == 1, part)
        pieces[d][:, :width] = first.astype(pieces[d].dtype)
        pieces[d ^ 1][:, width:] = second.astype(pieces[d ^ 1].dtype)
    for move in moves:
        move.wait()


def transfer_kernel(
    transfer, inverse_own, inverse_got, after, transfer_out, transfer_own, turned, raw, sems,
):
    rows, nonzero, half = transfer_own.shape[:3]
    mine = (lax.axis_index("sec") & 1) * half
    targets = [(transfer_out, half - mine), (transfer_own, mine)]
    copies = [
        pltpu.make_async_copy(
            transfer.at[r, :, pl.ds(first, half)], raw.at[n * rows + r], sems.at[n * rows + r]
        )
        for n, (_, first) in enumerate(targets)
        for r in range(rows)
    ]
    for copy in copies:
        copy.start()
    for r in range(rows):
        for f in range(half):
            turned[r, f] = inverse_own[r, f].T
            turned[rows + r, f] = inverse_got[r, f].T
    for n, (target, _) in enumerate(targets):
        for r in range(rows):
            copies[n * rows + r].wait()
            for k in range(nonzero):
                for f in range(half):
                    target[r, k, f] = raw[n * rows + r, k, f].T


def initial_kernel(own, got1, got2, got3, inverse_own, inverse_got, after, load, initial, passed):
    part, freqs, block, _ = inverse_own.shape
    for r in range(2 * part):
        inverse = inverse_own if r < part else inverse_got
        cols = slice(r * block, (r + 1) * block)
        total = own[:, cols] + got1[:, cols].astype(jnp.float32)
        total += got2[:, cols].astype(jnp.float32) + got3[:, cols].astype(jnp.float32)
        load[:, cols] = total
        solved = nt_dot(total.astype(jnp.bfloat16), inverse[r % part].reshape(freqs * block, block))
        initial[:, cols] = diagonal(solved, freqs).astype(jnp.bfloat16)


def step_kernel(
    step, chosen, far, near, previous, load,
    transfer_own, transfer_got, inverse, cols_own, cols_got, out, state, ids, sems,
):
    part, nonzero, freqs, block, _ = transfer_own.shape
    rows = 2 * part
    sec = lax.axis_index("sec")
    bay = lax.axis_index("bay")

    @pl.when(bay == step)
    def _():
        copies = [
            pltpu.make_async_copy(cols, ids.at[n], sems.at[n]) for n, cols in enumerate((cols_own, cols_got))
        ]
        for copy in copies:
            copy.start()
        for n in range(2):
            source = (near, far)[n]
            for r in range(rows):
                home = (sec ^ (2 * n + r // part)) * part + r % part
                state[home] = source[:, r * block:(r + 1) * block]
        for copy in copies:
            copy.wait()
        for r in chosen:
            cols = slice(r * block, (r + 1) * block)
            goal = slice((r - chosen[0]) * block, (r - chosen[0] + 1) * block)
            transfer = transfer_own if r < part else transfer_got
            picked = jnp.concatenate([state[ids[r // part, r % part, 0, k]] for k in range(nonzero)], axis=1)
            matrix = jnp.concatenate(
                [jnp.concatenate([transfer[r % part, k, f] for f in range(freqs)], axis=1) for k in range(nonzero)],
                axis=0,
            )
            summed = (load[:, cols] + diagonal(nn_dot(picked, matrix), freqs)).astype(jnp.bfloat16)
            solved = nn_dot(summed, jnp.concatenate([inverse[r, f] for f in range(freqs)], axis=1))
            out[:, goal] = diagonal(solved, freqs).astype(jnp.bfloat16)

    @pl.when(bay != step)
    def _():
        out[...] = previous[:, chosen[0] * block:(chosen[-1] + 1) * block]


def finish_kernel(kept, got, out):
    lines, width = got.shape
    odd = (lax.axis_index("sec") & 1) == 1

    @pl.when(odd)
    def _():
        out[:lines] = got[...]
        out[lines:] = kept[...]

    @pl.when(jnp.logical_not(odd))
    def _():
        out[:lines] = kept[...]
        out[lines:] = got[...]


def in_hbm(value):
    return pltpu.with_memory_space_constraint(value, pltpu.HBM)


def moved(value, distance, offset):
    bays, secs = lax.axis_size("bay"), lax.axis_size("sec")
    route = [
        (b * secs + s, (b + distance) % bays * secs + (s ^ offset))
        for b in range(bays)
        for s in range(secs)
    ]
    return lax.ppermute(value, ("bay", "sec"), route)


def hop(value, source, offset):
    bays, secs = lax.axis_size("bay"), lax.axis_size("sec")
    target = (source + 1) % bays
    cycle = list(range(bays))
    if bays > 3 and target == 1:
        cycle = [0, 1, 3, 2]
    elif bays > 3 and target > 1:
        cycle = [source, target, target + 1 if target + 1 < bays else source - 1]
    goes = {b: cycle[(n + 1) % len(cycle)] for n, b in enumerate(cycle)}
    route = [
        (b * secs + s, goes[b] * secs + (s ^ offset) if b in goes else b * secs + (s ^ 1))
        for b in range(bays)
        for s in range(secs)
    ]
    return lax.ppermute(value, ("bay", "sec"), route)


def per_device(edge_load, interior_load, coupling, block_cols, transfer, local_inverse):
    _, freqs, cases, width = edge_load.shape
    _, rows, nonzero, _, block, _ = transfer.shape
    inner = interior_load.shape[-1]
    half = freqs // 2
    lines = half * cases
    bays = lax.axis_size("bay")
    edge = edge_load.reshape(freqs * cases, width)
    interior = interior_load.reshape(freqs * cases, inner)
    params = pltpu.CompilerParams(vmem_limit_bytes=20 * MIB)
    bf16, f32 = jnp.bfloat16, jnp.float32
    wide = (lines, 2 * width)
    matrices = (rows, nonzero, half, block, block)
    inverses = (rows, half, block, block)

    cols_own = jnp.transpose(block_cols, (1, 0, 2))
    piece1, piece2, piece3, own, inverse_own, inverse_out = pl.pallas_call(
        force_kernel,
        out_shape=[jax.ShapeDtypeStruct(wide, bf16)] * 3
        + [jax.ShapeDtypeStruct(wide, f32)]
        + [pltpu.VMEM(inverses, bf16)] * 2,
        in_specs=[ANY] * 4,
        out_specs=[VMEM] * 6,
        scratch_shapes=[
            pltpu.VMEM((2, 2 * lines, inner), bf16),
            pltpu.VMEM((4, inner, width), bf16),
            pltpu.SemaphoreType.DMA((8,)),
        ],
        compiler_params=params,
        name="force",
    )(in_hbm(interior), in_hbm(edge), in_hbm(coupling[0]), in_hbm(local_inverse[0]))
    got2, got3, got1 = moved(piece2, 0, 2), moved(piece3, 0, 3), moved(piece1, 0, 1)
    inverse_got = moved(inverse_out, 0, 1)
    cols_got = moved(cols_own, 0, 1)

    transfer_out, transfer_own, turned = pl.pallas_call(
        transfer_kernel,
        out_shape=[pltpu.VMEM(matrices, bf16)] * 2
        + [pltpu.VMEM((2 * rows,) + inverses[1:], bf16)],
        in_specs=[ANY, VMEM, VMEM, ANY],
        out_specs=[VMEM] * 3,
        scratch_shapes=[
            pltpu.VMEM((2 * rows,) + matrices[1:], bf16),
            pltpu.SemaphoreType.DMA((2 * rows,)),
        ],
        compiler_params=params,
        name="transfer",
    )(in_hbm(transfer[0]), inverse_own, inverse_got, got1)
    load, state, transfer_out = pl.pallas_call(
        initial_kernel,
        out_shape=[
            jax.ShapeDtypeStruct(wide, f32),
            jax.ShapeDtypeStruct(wide, bf16),
            pltpu.VMEM(matrices, bf16),
        ],
        in_specs=[VMEM] * 6 + [ANY],
        out_specs=[VMEM, VMEM, ANY],
        input_output_aliases={6: 2},
        compiler_params=params,
        name="initial",
    )(own, got1, got2, got3, inverse_own, inverse_got, transfer_out)
    transfer_got = moved(transfer_out, 0, 1)

    def advance(step, chosen, far, near, state):
        return pl.pallas_call(
            functools.partial(step_kernel, step, chosen),
            out_shape=jax.ShapeDtypeStruct((lines, len(chosen) * block), bf16),
            in_specs=[VMEM] * 9,
            out_specs=VMEM,
            scratch_shapes=[
                pltpu.VMEM((4 * rows, lines, block), bf16),
                pltpu.SMEM((2,) + cols_own.shape, jnp.int32),
                pltpu.SemaphoreType.DMA((2,)),
            ],
            compiler_params=params,
            name="step",
        )(far, near, state, load, transfer_own, transfer_got, turned, cols_own, cols_got)

    for step in range(bays):
        source = (step - 1) % bays
        far = hop(state, source, 2)
        near = hop(state, source, 0)
        if step + 1 < bays:
            state = advance(step, range(2 * rows), far, near, state)
    got = moved(advance(bays - 1, range(rows, 2 * rows), far, near, state), 0, 1)
    kept = advance(bays - 1, range(rows), far, near, state)
    result = pl.pallas_call(
        finish_kernel,
        out_shape=jax.ShapeDtypeStruct((2 * lines, width), bf16),
        in_specs=[VMEM, VMEM],
        out_specs=VMEM,
        compiler_params=params,
        name="finish",
    )(kept, got)
    return result.reshape(1, freqs, cases, width)


def solution(mesh):
    in_specs = (
        P(("groups", "bay"), None, None, "sec"),
        P(("groups", "bay"), None, None, "sec"),
        P(("groups", "bay"), "sec", None),
        P(("groups", "bay"), "sec", None),
        P(("groups", "bay"), "sec", None, None, None, None),
        P(("groups", "bay"), "sec", None, None, None),
    )
    out_specs = P(("groups", "bay"), None, None, "sec")
    return jax.shard_map(
        per_device, mesh=mesh, in_specs=in_specs, out_specs=out_specs, check_vma=False
    )
```

```python
import functools

import jax
import jax.numpy as jnp
from jax import lax
from jax.experimental import pallas as pl
from jax.experimental.pallas import tpu as pltpu
from jax.sharding import PartitionSpec as P

VMEM = pl.BlockSpec(memory_space=pltpu.VMEM)
SMEM = pl.BlockSpec(memory_space=pltpu.SMEM)
ANY = pl.BlockSpec(memory_space=pl.ANY)
MIB = 1 << 20


def nt_dot(left, right):
    return lax.dot_general(left, right, (((1,), (1,)), ((), ())), preferred_element_type=jnp.float32)


def nn_dot(left, right):
    return jnp.dot(left, right, preferred_element_type=jnp.float32)


def diagonal(product, freqs):
    rows, cols = product.shape[0] // freqs, product.shape[1] // freqs
    return jnp.concatenate(
        [product[f * rows:(f + 1) * rows, f * cols:(f + 1) * cols] for f in range(freqs)], axis=0
    )


def by_parity(odd, rows):
    half = rows.shape[0] // 2
    return jnp.where(odd, rows[half:], rows[:half]), jnp.where(odd, rows[:half], rows[half:])


def columns_of(coupling, owner, width):
    return coupling.at[:, pl.ds(pl.multiple_of(owner * width, width), width)]


def force_kernel(
    interior, edge, coupling, inverse,
    piece1, piece2, piece3, own, inverse_own, inverse_out, loads, held, sems,
):
    sec = lax.axis_index("sec")
    width = held.shape[-1]
    half = inverse.shape[1] // 2
    mine = (sec & 1) * half
    loads_in = pltpu.make_async_copy(interior, loads.at[0], sems.at[4])
    edge_in = pltpu.make_async_copy(edge, loads.at[1], sems.at[5])
    loads_in.start()
    order = (2, 3, 1, 0)
    copies = [
        pltpu.make_async_copy(columns_of(coupling, sec ^ d, width), held.at[n], sems.at[n])
        for n, d in enumerate(order)
    ]
    for copy in copies:
        copy.start()
    edge_in.start()
    moves = [
        pltpu.make_async_copy(inverse.at[:, pl.ds(half - mine, half)], inverse_out, sems.at[6]),
        pltpu.make_async_copy(inverse.at[:, pl.ds(mine, half)], inverse_own, sems.at[7]),
    ]
    for move in moves:
        move.start()
    loads_in.wait()
    pieces = (own, piece1, piece2, piece3)
    for n, d in enumerate(order):
        copies[n].wait()
        part = -jnp.dot(loads[0], held[n], preferred_element_type=jnp.float32)
        if d == 0:
            edge_in.wait()
            part += loads[1].astype(jnp.float32)
        first, second = by_parity(((sec ^ d) & 1) == 1, part)
        pieces[d][:, :width] = first.astype(pieces[d].dtype)
        pieces[d ^ 1][:, width:] = second.astype(pieces[d ^ 1].dtype)
    for move in moves:
        move.wait()


def transfer_kernel(
    transfer, inverse_own, inverse_got, after, transfer_out, transfer_own, turned, raw, sems,
):
    rows, nonzero, half = transfer_own.shape[:3]
    mine = (lax.axis_index("sec") & 1) * half
    targets = [(transfer_out, half - mine), (transfer_own, mine)]
    copies = [
        pltpu.make_async_copy(
            transfer.at[r, :, pl.ds(first, half)], raw.at[n * rows + r], sems.at[n * rows + r]
        )
        for n, (_, first) in enumerate(targets)
        for r in range(rows)
    ]
    for copy in copies:
        copy.start()
    for r in range(rows):
        for f in range(half):
            turned[r, f] = inverse_own[r, f].T
            turned[rows + r, f] = inverse_got[r, f].T
    for n, (target, _) in enumerate(targets):
        for r in range(rows):
            copies[n * rows + r].wait()
            for k in range(nonzero):
                for f in range(half):
                    target[r, k, f] = raw[n * rows + r, k, f].T


def initial_kernel(own, got1, got2, got3, inverse_own, inverse_got, after, load, initial, passed):
    part, freqs, block, _ = inverse_own.shape
    for r in range(2 * part):
        inverse = inverse_own if r < part else inverse_got
        cols = slice(r * block, (r + 1) * block)
        total = own[:, cols] + got1[:, cols].astype(jnp.float32)
        total += got2[:, cols].astype(jnp.float32) + got3[:, cols].astype(jnp.float32)
        load[:, cols] = total
        solved = nt_dot(total.astype(jnp.bfloat16), inverse[r % part].reshape(freqs * block, block))
        initial[:, cols] = diagonal(solved, freqs).astype(jnp.bfloat16)


def step_kernel(
    step, chosen, far, near, previous, load,
    transfer_own, transfer_got, inverse, cols_own, cols_got, out, state, sums, ids, sems,
):
    part, nonzero, freqs, block, _ = transfer_own.shape
    rows = 2 * part
    sec = lax.axis_index("sec")
    bay = lax.axis_index("bay")

    @pl.when(bay == step)
    def _():
        copies = [
            pltpu.make_async_copy(cols, ids.at[n], sems.at[n]) for n, cols in enumerate((cols_own, cols_got))
        ]
        for copy in copies:
            copy.start()
        for r in chosen:
            cols = slice(r * block, (r + 1) * block)
            transfer = transfer_own if r < part else transfer_got
            first = jnp.concatenate([transfer[r % part, 0, f] for f in range(freqs)], axis=1)
            sums[:, cols] = load[:, cols] + diagonal(nn_dot(near[:, cols], first), freqs)
        for n in range(2):
            source = (near, far)[n]
            for r in range(rows):
                home = (sec ^ (2 * n + r // part)) * part + r % part
                state[home] = source[:, r * block:(r + 1) * block]
        for copy in copies:
            copy.wait()
        for r in chosen:
            cols = slice(r * block, (r + 1) * block)
            goal = slice((r - chosen[0]) * block, (r - chosen[0] + 1) * block)
            transfer = transfer_own if r < part else transfer_got
            picked = jnp.concatenate([state[ids[r // part, r % part, 0, k]] for k in range(1, nonzero)], axis=1)
            matrix = jnp.concatenate(
                [jnp.concatenate([transfer[r % part, k, f] for f in range(freqs)], axis=1) for k in range(1, nonzero)],
                axis=0,
            )
            summed = (sums[:, cols] + diagonal(nn_dot(picked, matrix), freqs)).astype(jnp.bfloat16)
            solved = nn_dot(summed, jnp.concatenate([inverse[r, f] for f in range(freqs)], axis=1))
            out[:, goal] = diagonal(solved, freqs).astype(jnp.bfloat16)

    @pl.when(bay != step)
    def _():
        out[...] = previous[:, chosen[0] * block:(chosen[-1] + 1) * block]


def finish_kernel(kept, got, out):
    lines, width = got.shape
    odd = (lax.axis_index("sec") & 1) == 1

    @pl.when(odd)
    def _():
        out[:lines] = got[...]
        out[lines:] = kept[...]

    @pl.when(jnp.logical_not(odd))
    def _():
        out[:lines] = kept[...]
        out[lines:] = got[...]


def in_hbm(value):
    return pltpu.with_memory_space_constraint(value, pltpu.HBM)


def moved(value, distance, offset):
    bays, secs = lax.axis_size("bay"), lax.axis_size("sec")
    route = [
        (b * secs + s, (b + distance) % bays * secs + (s ^ offset))
        for b in range(bays)
        for s in range(secs)
    ]
    return lax.ppermute(value, ("bay", "sec"), route)


def hop(value, source, offset):
    bays, secs = lax.axis_size("bay"), lax.axis_size("sec")
    target = (source + 1) % bays
    cycle = list(range(bays))
    if bays > 3 and target == 1:
        cycle = [0, 1, 3, 2]
    elif bays > 3 and target > 1:
        after = target + 1 if target + 1 < bays else 0 if offset else source - 1
        cycle = [source, target, after]
    goes = {b: cycle[(n + 1) % len(cycle)] for n, b in enumerate(cycle)}
    route = [
        (b * secs + s, goes[b] * secs + (s ^ offset) if b in goes else b * secs + (s ^ 1))
        for b in range(bays)
        for s in range(secs)
    ]
    return lax.ppermute(value, ("bay", "sec"), route)


def per_device(edge_load, interior_load, coupling, block_cols, transfer, local_inverse):
    _, freqs, cases, width = edge_load.shape
    _, rows, nonzero, _, block, _ = transfer.shape
    inner = interior_load.shape[-1]
    half = freqs // 2
    lines = half * cases
    bays = lax.axis_size("bay")
    edge = edge_load.reshape(freqs * cases, width)
    interior = interior_load.reshape(freqs * cases, inner)
    params = pltpu.CompilerParams(vmem_limit_bytes=20 * MIB)
    bf16, f32 = jnp.bfloat16, jnp.float32
    wide = (lines, 2 * width)
    matrices = (rows, nonzero, half, block, block)
    inverses = (rows, half, block, block)

    cols_own = jnp.transpose(block_cols, (1, 0, 2))
    piece1, piece2, piece3, own, inverse_own, inverse_out = pl.pallas_call(
        force_kernel,
        out_shape=[jax.ShapeDtypeStruct(wide, bf16)] * 3
        + [jax.ShapeDtypeStruct(wide, f32)]
        + [pltpu.VMEM(inverses, bf16)] * 2,
        in_specs=[ANY] * 4,
        out_specs=[VMEM] * 6,
        scratch_shapes=[
            pltpu.VMEM((2, 2 * lines, inner), bf16),
            pltpu.VMEM((4, inner, width), bf16),
            pltpu.SemaphoreType.DMA((8,)),
        ],
        compiler_params=params,
        name="force",
    )(in_hbm(interior), in_hbm(edge), in_hbm(coupling[0]), in_hbm(local_inverse[0]))
    got2, got3, got1 = moved(piece2, 0, 2), moved(piece3, 0, 3), moved(piece1, 0, 1)
    inverse_got = moved(inverse_out, 0, 1)
    cols_got = moved(cols_own, 0, 1)

    transfer_out, transfer_own, turned = pl.pallas_call(
        transfer_kernel,
        out_shape=[pltpu.VMEM(matrices, bf16)] * 2
        + [pltpu.VMEM((2 * rows,) + inverses[1:], bf16)],
        in_specs=[ANY, VMEM, VMEM, ANY],
        out_specs=[VMEM] * 3,
        scratch_shapes=[
            pltpu.VMEM((2 * rows,) + matrices[1:], bf16),
            pltpu.SemaphoreType.DMA((2 * rows,)),
        ],
        compiler_params=params,
        name="transfer",
    )(in_hbm(transfer[0]), inverse_own, inverse_got, got1)
    load, state, transfer_out = pl.pallas_call(
        initial_kernel,
        out_shape=[
            jax.ShapeDtypeStruct(wide, f32),
            jax.ShapeDtypeStruct(wide, bf16),
            pltpu.VMEM(matrices, bf16),
        ],
        in_specs=[VMEM] * 6 + [ANY],
        out_specs=[VMEM, VMEM, ANY],
        input_output_aliases={6: 2},
        compiler_params=params,
        name="initial",
    )(own, got1, got2, got3, inverse_own, inverse_got, transfer_out)
    transfer_got = moved(transfer_out, 0, 1)

    def advance(step, chosen, far, near, state):
        return pl.pallas_call(
            functools.partial(step_kernel, step, chosen),
            out_shape=jax.ShapeDtypeStruct((lines, len(chosen) * block), bf16),
            in_specs=[VMEM] * 9,
            out_specs=VMEM,
            scratch_shapes=[
                pltpu.VMEM((4 * rows, lines, block), bf16),
                pltpu.VMEM(wide, f32),
                pltpu.SMEM((2,) + cols_own.shape, jnp.int32),
                pltpu.SemaphoreType.DMA((2,)),
            ],
            compiler_params=params,
            name="step",
        )(far, near, state, load, transfer_own, transfer_got, turned, cols_own, cols_got)

    for step in range(bays):
        source = (step - 1) % bays
        far = hop(state, source, 2)
        near = hop(state, source, 0)
        if step + 1 < bays:
            state = advance(step, range(2 * rows), far, near, state)
    got = moved(advance(bays - 1, range(rows, 2 * rows), far, near, state), 0, 1)
    kept = advance(bays - 1, range(rows), far, near, state)
    result = pl.pallas_call(
        finish_kernel,
        out_shape=jax.ShapeDtypeStruct((2 * lines, width), bf16),
        in_specs=[VMEM, VMEM],
        out_specs=VMEM,
        compiler_params=params,
        name="finish",
    )(kept, got)
    return result.reshape(1, freqs, cases, width)


def solution(mesh):
    in_specs = (
        P(("groups", "bay"), None, None, "sec"),
        P(("groups", "bay"), None, None, "sec"),
        P(("groups", "bay"), "sec", None),
        P(("groups", "bay"), "sec", None),
        P(("groups", "bay"), "sec", None, None, None, None),
        P(("groups", "bay"), "sec", None, None, None),
    )
    out_specs = P(("groups", "bay"), None, None, "sec")
    return jax.shard_map(
        per_device, mesh=mesh, in_specs=in_specs, out_specs=out_specs, check_vma=False
    )
```

```python
import functools

import jax
import jax.numpy as jnp
from jax import lax
from jax.experimental import pallas as pl
from jax.experimental.pallas import tpu as pltpu
from jax.sharding import PartitionSpec as P

VMEM = pl.BlockSpec(memory_space=pltpu.VMEM)
SMEM = pl.BlockSpec(memory_space=pltpu.SMEM)
ANY = pl.BlockSpec(memory_space=pl.ANY)
MIB = 1 << 20


def nt_dot(left, right):
    return lax.dot_general(left, right, (((1,), (1,)), ((), ())), preferred_element_type=jnp.float32)


def nn_dot(left, right):
    return jnp.dot(left, right, preferred_element_type=jnp.float32)


def beside(first, second):
    return jnp.concatenate(
        [
            jnp.concatenate([first, jnp.zeros_like(second)], axis=1),
            jnp.concatenate([jnp.zeros_like(first), second], axis=1),
        ],
        axis=0,
    )


def diagonal(product, freqs):
    rows, cols = product.shape[0] // freqs, product.shape[1] // freqs
    return jnp.concatenate(
        [product[f * rows:(f + 1) * rows, f * cols:(f + 1) * cols] for f in range(freqs)], axis=0
    )


def by_parity(odd, rows):
    half = rows.shape[0] // 2
    return jnp.where(odd, rows[half:], rows[:half]), jnp.where(odd, rows[:half], rows[half:])


def columns_of(coupling, owner, width):
    return coupling.at[:, pl.ds(pl.multiple_of(owner * width, width), width)]


def force_kernel(
    interior, edge, coupling, inverse,
    piece1, piece2, piece3, own, inverse_own, inverse_out, loads, held, sems,
):
    sec = lax.axis_index("sec")
    width = held.shape[-1]
    half = inverse.shape[1] // 2
    mine = (sec & 1) * half
    loads_in = pltpu.make_async_copy(interior, loads.at[0], sems.at[4])
    edge_in = pltpu.make_async_copy(edge, loads.at[1], sems.at[5])
    loads_in.start()
    order = (2, 3, 1, 0)
    copies = [
        pltpu.make_async_copy(columns_of(coupling, sec ^ d, width), held.at[n], sems.at[n])
        for n, d in enumerate(order)
    ]
    for copy in copies:
        copy.start()
    edge_in.start()
    moves = [
        pltpu.make_async_copy(inverse.at[:, pl.ds(half - mine, half)], inverse_out, sems.at[6]),
        pltpu.make_async_copy(inverse.at[:, pl.ds(mine, half)], inverse_own, sems.at[7]),
    ]
    for move in moves:
        move.start()
    loads_in.wait()
    pieces = (own, piece1, piece2, piece3)
    for n, d in enumerate(order):
        copies[n].wait()
        part = -jnp.dot(loads[0], held[n], preferred_element_type=jnp.float32)
        if d == 0:
            edge_in.wait()
            part += loads[1].astype(jnp.float32)
        first, second = by_parity(((sec ^ d) & 1) == 1, part)
        pieces[d][:, :width] = first.astype(pieces[d].dtype)
        pieces[d ^ 1][:, width:] = second.astype(pieces[d ^ 1].dtype)
    for move in moves:
        move.wait()


def transfer_kernel(
    transfer, inverse_own, inverse_got, after, transfer_out, transfer_own, turned, raw, sems,
):
    rows, nonzero, half = transfer_own.shape[:3]
    mine = (lax.axis_index("sec") & 1) * half
    targets = [(transfer_out, half - mine), (transfer_own, mine)]
    copies = [
        pltpu.make_async_copy(
            transfer.at[r, :, pl.ds(first, half)], raw.at[n * rows + r], sems.at[n * rows + r]
        )
        for n, (_, first) in enumerate(targets)
        for r in range(rows)
    ]
    for copy in copies:
        copy.start()
    for r in range(rows):
        for f in range(half):
            turned[r, f] = inverse_own[r, f].T
            turned[rows + r, f] = inverse_got[r, f].T
    for n, (target, _) in enumerate(targets):
        for r in range(rows):
            copies[n * rows + r].wait()
            for k in range(nonzero):
                for f in range(half):
                    target[r, k, f] = raw[n * rows + r, k, f].T


def initial_kernel(own, got1, got2, got3, inverse_own, inverse_got, after, load, initial, passed):
    part, freqs, block, _ = inverse_own.shape
    for r in range(2 * part):
        inverse = inverse_own if r < part else inverse_got
        cols = slice(r * block, (r + 1) * block)
        total = own[:, cols] + got1[:, cols].astype(jnp.float32)
        total += got2[:, cols].astype(jnp.float32) + got3[:, cols].astype(jnp.float32)
        load[:, cols] = total
        solved = nt_dot(total.astype(jnp.bfloat16), inverse[r % part].reshape(freqs * block, block))
        initial[:, cols] = diagonal(solved, freqs).astype(jnp.bfloat16)


def step_kernel(
    step, chosen, far, near, previous, load,
    transfer_own, transfer_got, inverse, cols_own, cols_got, out, state, ids, sems,
):
    part, nonzero, freqs, block, _ = transfer_own.shape
    rows = 2 * part
    sec = lax.axis_index("sec")
    bay = lax.axis_index("bay")

    height = out.shape[0]

    def across(blocks, *place):
        return jnp.concatenate([blocks[(*place, f)] for f in range(freqs)], axis=1)

    def transfer_of(r):
        return transfer_own if r < part else transfer_got

    def solve(pair, summed):
        matrix = jnp.concatenate([across(inverse, n) for n in pair], axis=0)
        solved = nn_dot(beside(*summed), matrix)
        for i, n in enumerate(pair):
            goal = slice((n - chosen[0]) * block, (n - chosen[0] + 1) * block)
            out[:, goal] = diagonal(solved[i * height:(i + 1) * height], freqs).astype(jnp.bfloat16)

    @pl.when(bay == step)
    def _():
        copies = [
            pltpu.make_async_copy(cols, ids.at[n], sems.at[n]) for n, cols in enumerate((cols_own, cols_got))
        ]
        for copy in copies:
            copy.start()
        for n in range(2):
            source = (near, far)[n]
            for r in range(rows):
                home = (sec ^ (2 * n + r // part)) * part + r % part
                state[home] = source[:, r * block:(r + 1) * block]
        for copy in copies:
            copy.wait()
        for r in chosen[::2]:
            pair = (r, r + 1)
            spans = [slice(n * block, (n + 1) * block) for n in pair]
            summed = []
            for n, cols in zip(pair, spans):
                transfer = transfer_own if n < part else transfer_got
                picked = jnp.concatenate(
                    [state[ids[n // part, n % part, 0, k]] for k in range(nonzero)], axis=1
                )
                matrix = jnp.concatenate([across(transfer, n % part, k) for k in range(nonzero)], axis=0)
                summed.append((load[:, cols] + diagonal(nn_dot(picked, matrix), freqs)).astype(jnp.bfloat16))
            solve(pair, summed)

    @pl.when(bay != step)
    def _():
        out[...] = previous[:, chosen[0] * block:(chosen[-1] + 1) * block]


def finish_kernel(kept, got, out):
    lines, width = got.shape
    odd = (lax.axis_index("sec") & 1) == 1

    @pl.when(odd)
    def _():
        out[:lines] = got[...]
        out[lines:] = kept[...]

    @pl.when(jnp.logical_not(odd))
    def _():
        out[:lines] = kept[...]
        out[lines:] = got[...]


def in_hbm(value):
    return pltpu.with_memory_space_constraint(value, pltpu.HBM)


def moved(value, distance, offset):
    bays, secs = lax.axis_size("bay"), lax.axis_size("sec")
    route = [
        (b * secs + s, (b + distance) % bays * secs + (s ^ offset))
        for b in range(bays)
        for s in range(secs)
    ]
    return lax.ppermute(value, ("bay", "sec"), route)


def hop(value, source, offset):
    bays, secs = lax.axis_size("bay"), lax.axis_size("sec")
    target = (source + 1) % bays
    cycle = list(range(bays))
    if bays > 3 and target == 1:
        cycle = [0, 1, 3, 2]
    elif bays > 3 and target > 1:
        after = target + 1 if target + 1 < bays else 0 if offset else source - 1
        cycle = [source, target, after]
    goes = {b: cycle[(n + 1) % len(cycle)] for n, b in enumerate(cycle)}
    route = [
        (b * secs + s, goes[b] * secs + (s ^ offset) if b in goes else b * secs + (s ^ 1))
        for b in range(bays)
        for s in range(secs)
    ]
    return lax.ppermute(value, ("bay", "sec"), route)


def per_device(edge_load, interior_load, coupling, block_cols, transfer, local_inverse):
    _, freqs, cases, width = edge_load.shape
    _, rows, nonzero, _, block, _ = transfer.shape
    inner = interior_load.shape[-1]
    half = freqs // 2
    lines = half * cases
    bays = lax.axis_size("bay")
    edge = edge_load.reshape(freqs * cases, width)
    interior = interior_load.reshape(freqs * cases, inner)
    params = pltpu.CompilerParams(vmem_limit_bytes=20 * MIB)
    bf16, f32 = jnp.bfloat16, jnp.float32
    wide = (lines, 2 * width)
    matrices = (rows, nonzero, half, block, block)
    inverses = (rows, half, block, block)

    cols_own = jnp.transpose(block_cols, (1, 0, 2))
    piece1, piece2, piece3, own, inverse_own, inverse_out = pl.pallas_call(
        force_kernel,
        out_shape=[jax.ShapeDtypeStruct(wide, bf16)] * 3
        + [jax.ShapeDtypeStruct(wide, f32)]
        + [pltpu.VMEM(inverses, bf16)] * 2,
        in_specs=[ANY] * 4,
        out_specs=[VMEM] * 6,
        scratch_shapes=[
            pltpu.VMEM((2, 2 * lines, inner), bf16),
            pltpu.VMEM((4, inner, width), bf16),
            pltpu.SemaphoreType.DMA((8,)),
        ],
        compiler_params=params,
        name="force",
    )(in_hbm(interior), in_hbm(edge), in_hbm(coupling[0]), in_hbm(local_inverse[0]))
    got2, got3, got1 = moved(piece2, 0, 2), moved(piece3, 0, 3), moved(piece1, 0, 1)
    inverse_got = moved(inverse_out, 0, 1)
    cols_got = moved(cols_own, 0, 1)

    transfer_out, transfer_own, turned = pl.pallas_call(
        transfer_kernel,
        out_shape=[pltpu.VMEM(matrices, bf16)] * 2
        + [pltpu.VMEM((2 * rows,) + inverses[1:], bf16)],
        in_specs=[ANY, VMEM, VMEM, ANY],
        out_specs=[VMEM] * 3,
        scratch_shapes=[
            pltpu.VMEM((2 * rows,) + matrices[1:], bf16),
            pltpu.SemaphoreType.DMA((2 * rows,)),
        ],
        compiler_params=params,
        name="transfer",
    )(in_hbm(transfer[0]), inverse_own, inverse_got, got1)
    load, state, transfer_out = pl.pallas_call(
        initial_kernel,
        out_shape=[
            jax.ShapeDtypeStruct(wide, f32),
            jax.ShapeDtypeStruct(wide, bf16),
            pltpu.VMEM(matrices, bf16),
        ],
        in_specs=[VMEM] * 6 + [ANY],
        out_specs=[VMEM, VMEM, ANY],
        input_output_aliases={6: 2},
        compiler_params=params,
        name="initial",
    )(own, got1, got2, got3, inverse_own, inverse_got, transfer_out)
    transfer_got = moved(transfer_out, 0, 1)

    def advance(step, chosen, far, near, state):
        return pl.pallas_call(
            functools.partial(step_kernel, step, chosen),
            out_shape=jax.ShapeDtypeStruct((lines, len(chosen) * block), bf16),
            in_specs=[VMEM] * 9,
            out_specs=VMEM,
            scratch_shapes=[
                pltpu.VMEM((4 * rows, lines, block), bf16),
                pltpu.SMEM((2,) + cols_own.shape, jnp.int32),
                pltpu.SemaphoreType.DMA((2,)),
            ],
            compiler_params=params,
            name="step",
        )(far, near, state, load, transfer_own, transfer_got, turned, cols_own, cols_got)

    for step in range(bays):
        source = (step - 1) % bays
        far = hop(state, source, 2)
        near = hop(state, source, 0)
        if step + 1 < bays:
            state = advance(step, range(2 * rows), far, near, state)
    got = moved(advance(bays - 1, range(rows, 2 * rows), far, near, state), 0, 1)
    kept = advance(bays - 1, range(rows), far, near, state)
    result = pl.pallas_call(
        finish_kernel,
        out_shape=jax.ShapeDtypeStruct((2 * lines, width), bf16),
        in_specs=[VMEM, VMEM],
        out_specs=VMEM,
        compiler_params=params,
        name="finish",
    )(kept, got)
    return result.reshape(1, freqs, cases, width)


def solution(mesh):
    in_specs = (
        P(("groups", "bay"), None, None, "sec"),
        P(("groups", "bay"), None, None, "sec"),
        P(("groups", "bay"), "sec", None),
        P(("groups", "bay"), "sec", None),
        P(("groups", "bay"), "sec", None, None, None, None),
        P(("groups", "bay"), "sec", None, None, None),
    )
    out_specs = P(("groups", "bay"), None, None, "sec")
    return jax.shard_map(
        per_device, mesh=mesh, in_specs=in_specs, out_specs=out_specs, check_vma=False
    )
```

```python
import functools

import jax
import jax.numpy as jnp
from jax import lax
from jax.experimental import pallas as pl
from jax.experimental.pallas import tpu as pltpu
from jax.sharding import PartitionSpec as P

VMEM = pl.BlockSpec(memory_space=pltpu.VMEM)
SMEM = pl.BlockSpec(memory_space=pltpu.SMEM)
ANY = pl.BlockSpec(memory_space=pl.ANY)
MIB = 1 << 20


def nt_dot(left, right):
    return lax.dot_general(left, right, (((1,), (1,)), ((), ())), preferred_element_type=jnp.float32)


def nn_dot(left, right):
    return jnp.dot(left, right, preferred_element_type=jnp.float32)


def beside(first, second):
    return jnp.concatenate(
        [
            jnp.concatenate([first, jnp.zeros_like(second)], axis=1),
            jnp.concatenate([jnp.zeros_like(first), second], axis=1),
        ],
        axis=0,
    )


def diagonal(product, freqs):
    rows, cols = product.shape[0] // freqs, product.shape[1] // freqs
    return jnp.concatenate(
        [product[f * rows:(f + 1) * rows, f * cols:(f + 1) * cols] for f in range(freqs)], axis=0
    )


def by_parity(odd, rows):
    half = rows.shape[0] // 2
    return jnp.where(odd, rows[half:], rows[:half]), jnp.where(odd, rows[:half], rows[half:])


def columns_of(coupling, owner, width):
    return coupling.at[:, pl.ds(pl.multiple_of(owner * width, width), width)]


def force_kernel(
    interior, edge, coupling, inverse,
    piece1, piece2, piece3, own, inverse_own, inverse_out, loads, held, sems,
):
    sec = lax.axis_index("sec")
    width = held.shape[-1]
    half = inverse.shape[1] // 2
    mine = (sec & 1) * half
    loads_in = pltpu.make_async_copy(interior, loads.at[0], sems.at[4])
    edge_in = pltpu.make_async_copy(edge, loads.at[1], sems.at[5])
    loads_in.start()
    order = (2, 3, 1, 0)
    copies = [
        pltpu.make_async_copy(columns_of(coupling, sec ^ d, width), held.at[n], sems.at[n])
        for n, d in enumerate(order)
    ]
    for copy in copies:
        copy.start()
    edge_in.start()
    moves = [
        pltpu.make_async_copy(inverse.at[:, pl.ds(half - mine, half)], inverse_out, sems.at[6]),
        pltpu.make_async_copy(inverse.at[:, pl.ds(mine, half)], inverse_own, sems.at[7]),
    ]
    for move in moves:
        move.start()
    loads_in.wait()
    pieces = (own, piece1, piece2, piece3)
    for n, d in enumerate(order):
        copies[n].wait()
        part = -jnp.dot(loads[0], held[n], preferred_element_type=jnp.float32)
        if d == 0:
            edge_in.wait()
            part += loads[1].astype(jnp.float32)
        first, second = by_parity(((sec ^ d) & 1) == 1, part)
        pieces[d][:, :width] = first.astype(pieces[d].dtype)
        pieces[d ^ 1][:, width:] = second.astype(pieces[d ^ 1].dtype)
    for move in moves:
        move.wait()


def transfer_kernel(
    transfer, inverse_own, inverse_got, after, transfer_out, transfer_own, turned, raw, sems,
):
    rows, nonzero, half = transfer_own.shape[:3]
    mine = (lax.axis_index("sec") & 1) * half
    targets = [(transfer_out, half - mine), (transfer_own, mine)]
    copies = [
        pltpu.make_async_copy(
            transfer.at[r, :, pl.ds(first, half)], raw.at[n * rows + r], sems.at[n * rows + r]
        )
        for n, (_, first) in enumerate(targets)
        for r in range(rows)
    ]
    for copy in copies:
        copy.start()
    for r in range(rows):
        for f in range(half):
            turned[r, f] = inverse_own[r, f].T
            turned[rows + r, f] = inverse_got[r, f].T
    for n, (target, _) in enumerate(targets):
        for r in range(rows):
            copies[n * rows + r].wait()
            for k in range(nonzero):
                for f in range(half):
                    target[r, k, f] = raw[n * rows + r, k, f].T


def initial_kernel(own, got1, got2, got3, inverse_own, inverse_got, after, load, initial, passed):
    part, freqs, block, _ = inverse_own.shape
    for r in range(2 * part):
        inverse = inverse_own if r < part else inverse_got
        cols = slice(r * block, (r + 1) * block)
        total = own[:, cols] + got1[:, cols].astype(jnp.float32)
        total += got2[:, cols].astype(jnp.float32) + got3[:, cols].astype(jnp.float32)
        load[:, cols] = total
        solved = nt_dot(total.astype(jnp.bfloat16), inverse[r % part].reshape(freqs * block, block))
        initial[:, cols] = diagonal(solved, freqs).astype(jnp.bfloat16)


def step_kernel(
    step, chosen, far, near, previous, load,
    transfer_own, transfer_got, inverse, cols_own, cols_got, out, state, ids, sems,
):
    part, nonzero, freqs, block, _ = transfer_own.shape
    rows = 2 * part
    sec = lax.axis_index("sec")
    bay = lax.axis_index("bay")

    height = out.shape[0]

    def across(blocks, *place):
        return jnp.concatenate([blocks[(*place, f)] for f in range(freqs)], axis=1)

    def solve(pair, summed):
        matrix = jnp.concatenate([across(inverse, n) for n in pair], axis=0)
        solved = nn_dot(beside(*summed), matrix)
        for i, n in enumerate(pair):
            goal = slice((n - chosen[0]) * block, (n - chosen[0] + 1) * block)
            out[:, goal] = diagonal(solved[i * height:(i + 1) * height], freqs).astype(jnp.bfloat16)

    @pl.when(bay == step)
    def _():
        copies = [
            pltpu.make_async_copy(cols, ids.at[n], sems.at[n]) for n, cols in enumerate((cols_own, cols_got))
        ]
        for copy in copies:
            copy.start()
        for n in range(2):
            source = (near, far)[n]
            for r in range(rows):
                home = (sec ^ (2 * n + r // part)) * part + r % part
                state[home] = source[:, r * block:(r + 1) * block]
        for copy in copies:
            copy.wait()
        waiting = []
        for r in chosen[::2]:
            pair = (r, r + 1)
            summed = []
            for n in pair:
                cols = slice(n * block, (n + 1) * block)
                transfer = transfer_own if n < part else transfer_got
                picked = jnp.concatenate(
                    [state[ids[n // part, n % part, 0, k]] for k in range(nonzero)], axis=1
                )
                matrix = jnp.concatenate([across(transfer, n % part, k) for k in range(nonzero)], axis=0)
                summed.append((load[:, cols] + diagonal(nn_dot(picked, matrix), freqs)).astype(jnp.bfloat16))
            waiting.append((pair, summed))
            if len(waiting) > len(chosen):
                solve(*waiting.pop(0))
        for pair, summed in waiting:
            solve(pair, summed)

    @pl.when(bay != step)
    def _():
        out[...] = previous[:, chosen[0] * block:(chosen[-1] + 1) * block]


def finish_kernel(kept, got, out):
    lines, width = got.shape
    odd = (lax.axis_index("sec") & 1) == 1

    @pl.when(odd)
    def _():
        out[:lines] = got[...]
        out[lines:] = kept[...]

    @pl.when(jnp.logical_not(odd))
    def _():
        out[:lines] = kept[...]
        out[lines:] = got[...]


def in_hbm(value):
    return pltpu.with_memory_space_constraint(value, pltpu.HBM)


def moved(value, distance, offset):
    bays, secs = lax.axis_size("bay"), lax.axis_size("sec")
    route = [
        (b * secs + s, (b + distance) % bays * secs + (s ^ offset))
        for b in range(bays)
        for s in range(secs)
    ]
    return lax.ppermute(value, ("bay", "sec"), route)


def hop(value, source, offset):
    bays, secs = lax.axis_size("bay"), lax.axis_size("sec")
    target = (source + 1) % bays
    cycle = list(range(bays))
    if bays > 3 and target == 1:
        cycle = [0, 1, 3, 2]
    elif bays > 3 and target > 1:
        after = target + 1 if target + 1 < bays else 0 if offset else source - 1
        cycle = [source, target, after]
    goes = {b: cycle[(n + 1) % len(cycle)] for n, b in enumerate(cycle)}
    route = [
        (b * secs + s, goes[b] * secs + (s ^ offset) if b in goes else b * secs + (s ^ 1))
        for b in range(bays)
        for s in range(secs)
    ]
    return lax.ppermute(value, ("bay", "sec"), route)


def per_device(edge_load, interior_load, coupling, block_cols, transfer, local_inverse):
    _, freqs, cases, width = edge_load.shape
    _, rows, nonzero, _, block, _ = transfer.shape
    inner = interior_load.shape[-1]
    half = freqs // 2
    lines = half * cases
    bays = lax.axis_size("bay")
    edge = edge_load.reshape(freqs * cases, width)
    interior = interior_load.reshape(freqs * cases, inner)
    params = pltpu.CompilerParams(vmem_limit_bytes=20 * MIB)
    bf16, f32 = jnp.bfloat16, jnp.float32
    wide = (lines, 2 * width)
    matrices = (rows, nonzero, half, block, block)
    inverses = (rows, half, block, block)

    cols_own = jnp.transpose(block_cols, (1, 0, 2))
    piece1, piece2, piece3, own, inverse_own, inverse_out = pl.pallas_call(
        force_kernel,
        out_shape=[jax.ShapeDtypeStruct(wide, bf16)] * 3
        + [jax.ShapeDtypeStruct(wide, f32)]
        + [pltpu.VMEM(inverses, bf16)] * 2,
        in_specs=[ANY] * 4,
        out_specs=[VMEM] * 6,
        scratch_shapes=[
            pltpu.VMEM((2, 2 * lines, inner), bf16),
            pltpu.VMEM((4, inner, width), bf16),
            pltpu.SemaphoreType.DMA((8,)),
        ],
        compiler_params=params,
        name="force",
    )(in_hbm(interior), in_hbm(edge), in_hbm(coupling[0]), in_hbm(local_inverse[0]))
    got2, got3, got1 = moved(piece2, 0, 2), moved(piece3, 0, 3), moved(piece1, 0, 1)
    inverse_got = moved(inverse_out, 0, 1)
    cols_got = moved(cols_own, 0, 1)

    transfer_out, transfer_own, turned = pl.pallas_call(
        transfer_kernel,
        out_shape=[pltpu.VMEM(matrices, bf16)] * 2
        + [pltpu.VMEM((2 * rows,) + inverses[1:], bf16)],
        in_specs=[ANY, VMEM, VMEM, ANY],
        out_specs=[VMEM] * 3,
        scratch_shapes=[
            pltpu.VMEM((2 * rows,) + matrices[1:], bf16),
            pltpu.SemaphoreType.DMA((2 * rows,)),
        ],
        compiler_params=params,
        name="transfer",
    )(in_hbm(transfer[0]), inverse_own, inverse_got, got1)
    load, state, transfer_out = pl.pallas_call(
        initial_kernel,
        out_shape=[
            jax.ShapeDtypeStruct(wide, f32),
            jax.ShapeDtypeStruct(wide, bf16),
            pltpu.VMEM(matrices, bf16),
        ],
        in_specs=[VMEM] * 6 + [ANY],
        out_specs=[VMEM, VMEM, ANY],
        input_output_aliases={6: 2},
        compiler_params=params,
        name="initial",
    )(own, got1, got2, got3, inverse_own, inverse_got, transfer_out)
    transfer_got = moved(transfer_out, 0, 1)

    def advance(step, chosen, far, near, state):
        return pl.pallas_call(
            functools.partial(step_kernel, step, chosen),
            out_shape=jax.ShapeDtypeStruct((lines, len(chosen) * block), bf16),
            in_specs=[VMEM] * 9,
            out_specs=VMEM,
            scratch_shapes=[
                pltpu.VMEM((4 * rows, lines, block), bf16),
                pltpu.SMEM((2,) + cols_own.shape, jnp.int32),
                pltpu.SemaphoreType.DMA((2,)),
            ],
            compiler_params=params,
            name="step",
        )(far, near, state, load, transfer_own, transfer_got, turned, cols_own, cols_got)

    for step in range(bays):
        source = (step - 1) % bays
        far = hop(state, source, 2)
        near = hop(state, source, 0)
        if step + 1 < bays:
            state = advance(step, range(2 * rows), far, near, state)
    got = moved(advance(bays - 1, range(rows, 2 * rows), far, near, state), 0, 1)
    kept = advance(bays - 1, range(rows), far, near, state)
    result = pl.pallas_call(
        finish_kernel,
        out_shape=jax.ShapeDtypeStruct((2 * lines, width), bf16),
        in_specs=[VMEM, VMEM],
        out_specs=VMEM,
        compiler_params=params,
        name="finish",
    )(kept, got)
    return result.reshape(1, freqs, cases, width)


def solution(mesh):
    in_specs = (
        P(("groups", "bay"), None, None, "sec"),
        P(("groups", "bay"), None, None, "sec"),
        P(("groups", "bay"), "sec", None),
        P(("groups", "bay"), "sec", None),
        P(("groups", "bay"), "sec", None, None, None, None),
        P(("groups", "bay"), "sec", None, None, None),
    )
    out_specs = P(("groups", "bay"), None, None, "sec")
    return jax.shard_map(
        per_device, mesh=mesh, in_specs=in_specs, out_specs=out_specs, check_vma=False
    )
```

```python
import functools

import jax
import jax.numpy as jnp
from jax import lax
from jax.experimental import pallas as pl
from jax.experimental.pallas import tpu as pltpu
from jax.sharding import PartitionSpec as P

VMEM = pl.BlockSpec(memory_space=pltpu.VMEM)
SMEM = pl.BlockSpec(memory_space=pltpu.SMEM)
ANY = pl.BlockSpec(memory_space=pl.ANY)
MIB = 1 << 20


def nt_dot(left, right):
    return lax.dot_general(left, right, (((1,), (1,)), ((), ())), preferred_element_type=jnp.float32)


def nn_dot(left, right):
    return jnp.dot(left, right, preferred_element_type=jnp.float32)


def beside(first, second):
    return jnp.concatenate(
        [
            jnp.concatenate([first, jnp.zeros_like(second)], axis=1),
            jnp.concatenate([jnp.zeros_like(first), second], axis=1),
        ],
        axis=0,
    )


def diagonal(product, freqs):
    rows, cols = product.shape[0] // freqs, product.shape[1] // freqs
    return jnp.concatenate(
        [product[f * rows:(f + 1) * rows, f * cols:(f + 1) * cols] for f in range(freqs)], axis=0
    )


def by_parity(odd, rows):
    half = rows.shape[0] // 2
    return jnp.where(odd, rows[half:], rows[:half]), jnp.where(odd, rows[:half], rows[half:])


def columns_of(coupling, owner, width):
    return coupling.at[:, pl.ds(pl.multiple_of(owner * width, width), width)]


def force_kernel(
    interior, edge, coupling, inverse,
    piece1, piece2, piece3, own, inverse_own, inverse_out, loads, held, sems,
):
    sec = lax.axis_index("sec")
    width = held.shape[-1]
    half = inverse.shape[1] // 2
    mine = (sec & 1) * half
    loads_in = pltpu.make_async_copy(interior, loads.at[0], sems.at[4])
    edge_in = pltpu.make_async_copy(edge, loads.at[1], sems.at[5])
    loads_in.start()
    order = (2, 3, 1, 0)
    copies = [
        pltpu.make_async_copy(columns_of(coupling, sec ^ d, width), held.at[n], sems.at[n])
        for n, d in enumerate(order)
    ]
    for copy in copies:
        copy.start()
    edge_in.start()
    moves = [
        pltpu.make_async_copy(inverse.at[:, pl.ds(half - mine, half)], inverse_out, sems.at[6]),
        pltpu.make_async_copy(inverse.at[:, pl.ds(mine, half)], inverse_own, sems.at[7]),
    ]
    for move in moves:
        move.start()
    loads_in.wait()
    pieces = (own, piece1, piece2, piece3)
    for n, d in enumerate(order):
        copies[n].wait()
        part = -jnp.dot(loads[0], held[n], preferred_element_type=jnp.float32)
        if d == 0:
            edge_in.wait()
            part += loads[1].astype(jnp.float32)
        first, second = by_parity(((sec ^ d) & 1) == 1, part)
        pieces[d][:, :width] = first.astype(pieces[d].dtype)
        pieces[d ^ 1][:, width:] = second.astype(pieces[d ^ 1].dtype)
    for move in moves:
        move.wait()


def transfer_kernel(
    transfer, inverse_own, inverse_got, after, transfer_out, transfer_own, turned, raw, sems,
):
    rows, nonzero, half = transfer_own.shape[:3]
    mine = (lax.axis_index("sec") & 1) * half
    targets = [(transfer_out, half - mine), (transfer_own, mine)]
    copies = [
        pltpu.make_async_copy(
            transfer.at[r, :, pl.ds(first, half)], raw.at[n * rows + r], sems.at[n * rows + r]
        )
        for n, (_, first) in enumerate(targets)
        for r in range(rows)
    ]
    for copy in copies:
        copy.start()
    for r in range(rows):
        for f in range(half):
            turned[r, f] = inverse_own[r, f].T
            turned[rows + r, f] = inverse_got[r, f].T
    for n, (target, _) in enumerate(targets):
        for r in range(rows):
            copies[n * rows + r].wait()
            for k in range(nonzero):
                for f in range(half):
                    target[r, k, f] = raw[n * rows + r, k, f].T


def initial_kernel(own, got1, got2, got3, inverse_own, inverse_got, after, load, initial, passed):
    part, freqs, block, _ = inverse_own.shape
    for r in range(2 * part):
        inverse = inverse_own if r < part else inverse_got
        cols = slice(r * block, (r + 1) * block)
        total = own[:, cols] + got1[:, cols].astype(jnp.float32)
        total += got2[:, cols].astype(jnp.float32) + got3[:, cols].astype(jnp.float32)
        load[:, cols] = total
        solved = nt_dot(total.astype(jnp.bfloat16), inverse[r % part].reshape(freqs * block, block))
        initial[:, cols] = diagonal(solved, freqs).astype(jnp.bfloat16)


def step_kernel(
    step, chosen, far, near, previous, load,
    transfer_own, transfer_got, inverse, cols_own, cols_got, out, state, ids, sems,
):
    part, nonzero, freqs, block, _ = transfer_own.shape
    rows = 2 * part
    sec = lax.axis_index("sec")
    bay = lax.axis_index("bay")

    height = out.shape[0]

    def across(blocks, *place):
        return jnp.concatenate([blocks[(*place, f)] for f in range(freqs)], axis=1)

    def solve(pair, summed):
        matrix = jnp.concatenate([across(inverse, n) for n in pair], axis=0)
        solved = nn_dot(beside(*summed), matrix)
        for i, n in enumerate(pair):
            goal = slice((n - chosen[0]) * block, (n - chosen[0] + 1) * block)
            out[:, goal] = diagonal(solved[i * height:(i + 1) * height], freqs).astype(jnp.bfloat16)

    @pl.when(bay == step)
    def _():
        copies = [
            pltpu.make_async_copy(cols, ids.at[n], sems.at[n]) for n, cols in enumerate((cols_own, cols_got))
        ]
        for copy in copies:
            copy.start()
        for n in range(2):
            source = (near, far)[n]
            for r in range(rows):
                home = (sec ^ (2 * n + r // part)) * part + r % part
                state[home] = source[:, r * block:(r + 1) * block]
        for copy in copies:
            copy.wait()
        waiting = []
        for r in chosen[::2]:
            pair = (r, r + 1)
            summed = []
            for n in pair:
                cols = slice(n * block, (n + 1) * block)
                transfer = transfer_own if n < part else transfer_got
                picked = jnp.concatenate(
                    [state[ids[n // part, n % part, 0, k]] for k in range(nonzero)], axis=1
                )
                matrix = jnp.concatenate([across(transfer, n % part, k) for k in range(nonzero)], axis=0)
                summed.append((load[:, cols] + diagonal(nn_dot(picked, matrix), freqs)).astype(jnp.bfloat16))
            waiting.append((pair, summed))
            if len(waiting) > len(chosen):
                solve(*waiting.pop(0))
        for pair, summed in waiting:
            solve(pair, summed)

    @pl.when(bay != step)
    def _():
        out[...] = previous[:, chosen[0] * block:(chosen[-1] + 1) * block]


def finish_kernel(kept, got, out):
    lines, width = got.shape
    odd = (lax.axis_index("sec") & 1) == 1

    @pl.when(odd)
    def _():
        out[:lines] = got[...]
        out[lines:] = kept[...]

    @pl.when(jnp.logical_not(odd))
    def _():
        out[:lines] = kept[...]
        out[lines:] = got[...]


def in_hbm(value):
    return pltpu.with_memory_space_constraint(value, pltpu.HBM)


def moved(value, distance, offset):
    bays, secs = lax.axis_size("bay"), lax.axis_size("sec")
    route = [
        (b * secs + s, (b + distance) % bays * secs + (s ^ offset))
        for b in range(bays)
        for s in range(secs)
    ]
    return lax.ppermute(value, ("bay", "sec"), route)


def hop(value, source, offset):
    bays, secs = lax.axis_size("bay"), lax.axis_size("sec")
    target = (source + 1) % bays
    cycle = list(range(bays))
    if bays > 3 and target > 0:
        after = target + 1
        if target == 1:
            after = 2 if offset else 3
        elif after == bays:
            after = 0 if offset else source - 1
        cycle = [source, target, after]
    goes = {b: cycle[(n + 1) % len(cycle)] for n, b in enumerate(cycle)}
    route = [
        (b * secs + s, goes[b] * secs + (s ^ offset) if b in goes else b * secs + (s ^ 1))
        for b in range(bays)
        for s in range(secs)
    ]
    return lax.ppermute(value, ("bay", "sec"), route)


def per_device(edge_load, interior_load, coupling, block_cols, transfer, local_inverse):
    _, freqs, cases, width = edge_load.shape
    _, rows, nonzero, _, block, _ = transfer.shape
    inner = interior_load.shape[-1]
    half = freqs // 2
    lines = half * cases
    bays = lax.axis_size("bay")
    edge = edge_load.reshape(freqs * cases, width)
    interior = interior_load.reshape(freqs * cases, inner)
    params = pltpu.CompilerParams(vmem_limit_bytes=20 * MIB)
    bf16, f32 = jnp.bfloat16, jnp.float32
    wide = (lines, 2 * width)
    matrices = (rows, nonzero, half, block, block)
    inverses = (rows, half, block, block)

    cols_own = jnp.transpose(block_cols, (1, 0, 2))
    piece1, piece2, piece3, own, inverse_own, inverse_out = pl.pallas_call(
        force_kernel,
        out_shape=[jax.ShapeDtypeStruct(wide, bf16)] * 3
        + [jax.ShapeDtypeStruct(wide, f32)]
        + [pltpu.VMEM(inverses, bf16)] * 2,
        in_specs=[ANY] * 4,
        out_specs=[VMEM] * 6,
        scratch_shapes=[
            pltpu.VMEM((2, 2 * lines, inner), bf16),
            pltpu.VMEM((4, inner, width), bf16),
            pltpu.SemaphoreType.DMA((8,)),
        ],
        compiler_params=params,
        name="force",
    )(in_hbm(interior), in_hbm(edge), in_hbm(coupling[0]), in_hbm(local_inverse[0]))
    got2, got3, got1 = moved(piece2, 0, 2), moved(piece3, 0, 3), moved(piece1, 0, 1)
    inverse_got = moved(inverse_out, 0, 1)
    cols_got = moved(cols_own, 0, 1)

    transfer_out, transfer_own, turned = pl.pallas_call(
        transfer_kernel,
        out_shape=[pltpu.VMEM(matrices, bf16)] * 2
        + [pltpu.VMEM((2 * rows,) + inverses[1:], bf16)],
        in_specs=[ANY, VMEM, VMEM, ANY],
        out_specs=[VMEM] * 3,
        scratch_shapes=[
            pltpu.VMEM((2 * rows,) + matrices[1:], bf16),
            pltpu.SemaphoreType.DMA((2 * rows,)),
        ],
        compiler_params=params,
        name="transfer",
    )(in_hbm(transfer[0]), inverse_own, inverse_got, got1)
    load, state, transfer_out = pl.pallas_call(
        initial_kernel,
        out_shape=[
            jax.ShapeDtypeStruct(wide, f32),
            jax.ShapeDtypeStruct(wide, bf16),
            pltpu.VMEM(matrices, bf16),
        ],
        in_specs=[VMEM] * 6 + [ANY],
        out_specs=[VMEM, VMEM, ANY],
        input_output_aliases={6: 2},
        compiler_params=params,
        name="initial",
    )(own, got1, got2, got3, inverse_own, inverse_got, transfer_out)
    transfer_got = moved(transfer_out, 0, 1)

    def advance(step, chosen, far, near, state):
        return pl.pallas_call(
            functools.partial(step_kernel, step, chosen),
            out_shape=jax.ShapeDtypeStruct((lines, len(chosen) * block), bf16),
            in_specs=[VMEM] * 9,
            out_specs=VMEM,
            scratch_shapes=[
                pltpu.VMEM((4 * rows, lines, block), bf16),
                pltpu.SMEM((2,) + cols_own.shape, jnp.int32),
                pltpu.SemaphoreType.DMA((2,)),
            ],
            compiler_params=params,
            name="step",
        )(far, near, state, load, transfer_own, transfer_got, turned, cols_own, cols_got)

    for step in range(bays):
        source = (step - 1) % bays
        far = hop(state, source, 2)
        near = hop(state, source, 0)
        if step + 1 < bays:
            state = advance(step, range(2 * rows), far, near, state)
    got = moved(advance(bays - 1, range(rows, 2 * rows), far, near, state), 0, 1)
    kept = advance(bays - 1, range(rows), far, near, state)
    result = pl.pallas_call(
        finish_kernel,
        out_shape=jax.ShapeDtypeStruct((2 * lines, width), bf16),
        in_specs=[VMEM, VMEM],
        out_specs=VMEM,
        compiler_params=params,
        name="finish",
    )(kept, got)
    return result.reshape(1, freqs, cases, width)


def solution(mesh):
    in_specs = (
        P(("groups", "bay"), None, None, "sec"),
        P(("groups", "bay"), None, None, "sec"),
        P(("groups", "bay"), "sec", None),
        P(("groups", "bay"), "sec", None),
        P(("groups", "bay"), "sec", None, None, None, None),
        P(("groups", "bay"), "sec", None, None, None),
    )
    out_specs = P(("groups", "bay"), None, None, "sec")
    return jax.shard_map(
        per_device, mesh=mesh, in_specs=in_specs, out_specs=out_specs, check_vma=False
    )
```
